256 devices in a mesh: group: 16 (over y, z_hi), tensor: 16 (over x, z_lo, core).
Axes of the slice: x: 4, y: 4, z: 8 (z_hi: 4, z_lo: 2; z = z_hi * 2 + z_lo), core: 2. Of those that a mesh axis runs over, the one named last changes fastest.
Arguments:
- latents: float32 [4096, 6144], P('group', 'tensor'), may hold values from -8 to 8
- input_weights: bfloat16 [3, 6144, 4096], P(None, None, 'tensor'), may hold values from -1 to 1
- output_weights: bfloat16 [4096, 6144], P(None, 'tensor'), may hold values from -0.1875 to 0.1875
- position_table: bfloat16 [16, 6144], P(None, 'tensor'), may hold values from -4 to 4
- level_scale: float32 [32, 6144], P(None, 'tensor'), may hold values from -2 to 2
- step_sizes: float32 [32], replicated, may hold values from 0.5 to 2
- levels: int32 [16, 2], P('group'), may hold values from 0 to 31
- group_order: int32 [16], P('group'), may hold values from 0 to 15, as said below
- group_mask: int32 [16, 16], P('group'), may hold values from 0 to 1, as said below
Outputs:
- denoised: float32 [4096, 6144], P('group', 'tensor')
- velocity: bfloat16 [4096, 6144], P('group', 'tensor')
The draws below stay inside these ranges and needn't reach their ends.
Inputs may be any that keep to these rules, and one draw needn't show every extreme that they name: `group_order`: a permutation of the groups' places. group_mask[c, c] = 1; group_mask[c, j] = 0 where group_order[j] > group_order[c]; where group_order[j] < group_order[c] it may be 0 or 1.
All inputs are finite; a program needn't handle non-finite values.
Results may differ from the reference program's by a relative error of at most 0.017.
Values may be sent and summed in bfloat16 or wider, within the bound.
No kernel may reach another device: no remote copies, remote signals or barrier semaphores. Data moves between devices by JAX's collectives and lax.ppermute only.
A program may use at most 128 MiB of HBM per device.

```python
import math
import jax
import jax.numpy as jnp
from jax import lax

D = 6144
HD = 128
HEADS = 32
LEVELS = 32
STEPS = 2
GROUPS = 16
TOKENS = 4096


def place_groups(key):
    return jax.random.permutation(key, GROUPS).astype(jnp.int32)


def plant_signs(key):
    return jax.random.rademacher(jax.random.fold_in(key, 97), (D,), dtype=jnp.float32)


def draw_group_order(key, part):
    placed = place_groups(key)
    return placed


def draw_group_mask(key, part):
    placed = place_groups(key)
    key = jax.random.fold_in(key, 5)
    dropped = jax.random.randint(key, (GROUPS, GROUPS), 0, 4).astype(jnp.int32)
    earlier = placed[None, :] < placed[:, None]
    diagonal = jnp.eye(GROUPS, dtype=jnp.int32) > 0
    chosen = jnp.where(diagonal, 1, jnp.where(earlier & (dropped > 0), 1, 0))
    return chosen.astype(jnp.int32)


def draw_input_weights(key, part):
    sign_vector = plant_signs(key)
    key = jax.random.fold_in(key, 11)
    base_key, unit_key = jax.random.split(key)
    column_count = HEADS * HD
    base_draw = jnp.clip(jax.random.normal(base_key, (3, D, column_count), jnp.float32), -4.0, 4.0) / math.sqrt(D)
    unit_signs = jax.random.rademacher(unit_key, (column_count,), dtype=jnp.float32) / math.sqrt(HD)
    gain_product = 0.05 * math.sqrt(HD)
    query_gain = 2.0
    key_gain = gain_product / query_gain
    outer_plant = (sign_vector / math.sqrt(D))[:, None] * unit_signs[None, :]
    stacked = jnp.stack([base_draw[0] + query_gain * outer_plant, base_draw[1] + key_gain * outer_plant, base_draw[2]])
    return stacked.astype(jnp.bfloat16)


def draw_latents(key, part):
    sign_vector = plant_signs(key)
    key = jax.random.fold_in(key, 7)
    pick_key = jax.random.fold_in(key, 0)
    noise_key = jax.random.fold_in(key, 1)
    amount_key = jax.random.fold_in(key, 3)
    chosen_rows = jax.random.randint(pick_key, (TOKENS, 1), 0, 16) == 0
    noise_draw = jax.random.normal(noise_key, (TOKENS, D), jnp.float32)
    strength = jax.random.uniform(amount_key, (TOKENS, 1), jnp.float32, 2.0, 5.0)
    drawn = noise_draw
    aligned = strength * sign_vector[None, :] + noise_draw
    return jnp.clip(jnp.where(chosen_rows, aligned, drawn), -8.0, 8.0)


def plant(entries, key, least, largest):
    longest = entries.shape.index(max(entries.shape))
    spots = []
    for shift in (0, 1):
        where = [jax.random.randint(jax.random.fold_in(key, axis), (), 0, length) for axis, length in enumerate(entries.shape)]
        where[longest] = (where[longest] + shift) % entries.shape[longest]
        spots.append(tuple(where))
    return entries.at[spots[0]].set(least).at[spots[1]].set(largest)


def shard_levels(key, shape, shards, low, top_value):
    def one(position, parts):
        steps = jax.random.uniform(jax.random.fold_in(jax.random.fold_in(key, 6), position), (parts,), jnp.float32, low / len(shards), top_value / len(shards))
        return jnp.repeat(jnp.exp(steps), shape[position] // parts).reshape((-1,) + (1,) * (len(shape) - position - 1))

    gain = one(*shards[0])
    for cut in shards[1:]:
        gain = gain * one(*cut)
    return gain


def normal_values(own_key, shape, deviation, most, cuts=(), kind=jnp.bfloat16):
    array = deviation * jax.random.normal(own_key, shape, jnp.float32)
    if cuts:
        array = array * shard_levels(own_key, shape, cuts, -0.22, 0.18)
    return jnp.clip(array, -most, most).astype(kind)


def setup_inputs(seed: int = 0) -> dict:
    key_list = jax.random.split(jax.random.key(seed), 10)
    return {
        "latents": draw_latents(jax.random.fold_in(key_list[9], 71), 0),
        "input_weights": draw_input_weights(jax.random.fold_in(key_list[9], 71), 0),
        "output_weights": normal_values(key_list[2], (HEADS * HD, D), (HEADS * HD // 4) ** -0.5, 0.1875, ((1, 16),)),
        "position_table": normal_values(key_list[3], (GROUPS, D), 0.7, 4.0, ((1, 16),)),
        "level_scale": normal_values(key_list[4], (LEVELS, D), 0.4, 2.0, ((1, 16),), jnp.float32),
        "step_sizes": jnp.clip(jax.random.uniform(key_list[5], (LEVELS,), jnp.float32, 0.5, 2.0), 0.5, 2.0),
        "levels": plant(jax.random.randint(key_list[6], (GROUPS, STEPS), 0, LEVELS), jax.random.fold_in(key_list[6], 1), 0, LEVELS - 1).astype(jnp.int32),
        "group_order": draw_group_order(jax.random.fold_in(key_list[9], 71), 0),
        "group_mask": draw_group_mask(jax.random.fold_in(key_list[9], 71), 0),
    }


def reference(latents, input_weights, output_weights, position_table, level_scale, step_sizes, levels, group_order, group_mask):
    group_count = levels.shape[0]
    token_count = latents.shape[0] // group_count
    position_rows = jnp.repeat(position_table[group_order].astype(jnp.float32), token_count, axis=0)
    allowed = jnp.repeat(group_mask > 0, token_count, axis=1)
    denoised = latents
    velocity = jnp.zeros_like(latents)
    for step_index in range(STEPS):
        level_now = levels[:, step_index]
        shifted = denoised + position_rows
        inverse_rms = lax.rsqrt(lax.optimization_barrier(jnp.sum(shifted * shifted, axis=1, keepdims=True)) / D + 1e-06)
        factor = jnp.repeat(1.0 + level_scale[level_now], token_count, axis=0)
        modulated = (shifted * factor).astype(jnp.bfloat16)
        projected = []
        for slot_index in range(3):
            product = jnp.dot(modulated, input_weights[slot_index], preferred_element_type=jnp.float32)
            projected.append((product * inverse_rms).astype(jnp.bfloat16).reshape(-1, HEADS, HD))
        queries, keys_all, values_all = projected
        keys_wide = keys_all.astype(jnp.float32)
        values_wide = values_all.astype(jnp.float32)

        def attend(group_index):
            query_block = lax.dynamic_slice_in_dim(queries, group_index * token_count, token_count, 0).astype(jnp.float32)
            scores = jnp.einsum('qhe,khe->hqk', query_block, keys_wide) / math.sqrt(HD)
            valid_keys = allowed[group_index]
            scores = jnp.where(valid_keys[None, None, :], scores, -jnp.inf)
            weights = jax.nn.softmax(scores, axis=-1).astype(jnp.bfloat16)
            attended = jnp.einsum('hqk,khe->qhe', weights.astype(jnp.float32), values_wide)
            return attended.astype(jnp.bfloat16).reshape(token_count, HEADS * HD)
        attended = lax.map(attend, jnp.arange(group_count, dtype=jnp.int32)).reshape(-1, HEADS * HD)
        velocity = jnp.dot(attended, output_weights, preferred_element_type=jnp.float32)
        sizes_now = jnp.repeat(step_sizes[level_now], token_count)[:, None]
        denoised = denoised + sizes_now * velocity
    return (denoised, velocity.astype(jnp.bfloat16))
```

```python
import functools
import math

import jax
import jax.numpy as jnp
from jax import lax
from jax.experimental import pallas as pl
from jax.experimental.pallas import tpu as pltpu
from jax.sharding import PartitionSpec as P

D = 6144
HD = 128
STEPS = 2
TOK = 256
HALF = 128
FEAT = 384
COLS = 256
ROWS = 272
NEG = -1e30
F32 = jnp.float32
BF16 = jnp.bfloat16
VM = pl.BlockSpec(memory_space=pltpu.VMEM)
SM = pl.BlockSpec(memory_space=pltpu.SMEM)
MB = 1 << 20


def t_perm(move):
    pairs = []
    for t in range(16):
        x, l, c = move(t // 4, t // 2 % 2, t % 2)
        pairs.append((t, (x % 4) * 4 + l * 2 + c))
    return pairs


X_UP = t_perm(lambda x, l, c: (x + 1, l, c))
X_DOWN = t_perm(lambda x, l, c: (x - 1, l, c))
Z_SWAP = t_perm(lambda x, l, c: (x, 1 - l, c))
C_SWAP = t_perm(lambda x, l, c: (x, l, 1 - c))
Y_UP = [(g, ((g // 4 + 1) % 4) * 4 + g % 4) for g in range(16)]
Y_DOWN = [(g, ((g // 4 - 1) % 4) * 4 + g % 4) for g in range(16)]
Y_FAR = [(g, ((g // 4 + 2) % 4) * 4 + g % 4) for g in range(16)]


def head_perm(a, b):
    pairs = []
    for g in range(16):
        for t in range(16):
            y, h, c = g // 4, g % 4, t % 2
            to_h, to_c = 2 * c + (h + a) % 2, (h // 2 + b) % 2
            pairs.append((g * 16 + t, (y * 4 + to_h) * 16 + t - c + to_c))
    return pairs


PIECES = [(a, b) for a in range(2) for b in range(2)]
HEAD_PERMS = [head_perm(a, b) for a, b in PIECES]
BACK_PERMS = [[(j, i) for i, j in pairs] for pairs in HEAD_PERMS]
BOTH = ("group", "tensor")


def move_t(array, pairs):
    return lax.ppermute(array, "tensor", pairs)


def move_g(array, pairs):
    return lax.ppermute(array, "group", pairs)


def call(kernel, out_shape, in_specs, out_specs, grid=None, scratch=(), limit=16, flops=0, size=0):
    return pl.pallas_call(
        kernel,
        out_shape=out_shape,
        grid_spec=pltpu.PrefetchScalarGridSpec(
            num_scalar_prefetch=1,
            grid=grid or (1,),
            in_specs=in_specs,
            out_specs=out_specs,
            scratch_shapes=scratch,
        ),
        compiler_params=pltpu.CompilerParams(vmem_limit_bytes=limit * MB),
        cost_estimate=pl.CostEstimate(flops=flops, bytes_accessed=size, transcendentals=0),
    )


def sds(shape, dtype):
    return jax.ShapeDtypeStruct(shape, dtype)


def modulate(info, step, shifted_from, scale_ref, table_ref, out_ref):
    level = info[5 + step]
    place = info[7]
    table = table_ref[...].astype(F32)
    row_at = lax.broadcasted_iota(jnp.int32, table.shape, 0)
    position = jnp.sum(jnp.where(row_at == place, table, 0.0), axis=0, keepdims=True)
    shifted = shifted_from + position
    factor = 1.0 + scale_ref[pl.ds(level, 1), :]
    out_ref[0:TOK, :] = (shifted * factor).astype(BF16)
    squares = jnp.sum(shifted * shifted, axis=1, keepdims=True)
    lanes = jnp.transpose(jnp.broadcast_to(squares, (TOK, 128)))[0:16, :]
    high = lanes.astype(BF16)
    rest = lanes - high.astype(F32)
    middle = rest.astype(BF16)
    low = (rest - middle.astype(F32)).astype(BF16)
    at = lax.broadcasted_iota(jnp.int32, lanes.shape, 0)
    parts = jnp.where(
        at == 0,
        high.astype(F32),
        jnp.where(at == 1, middle.astype(F32), jnp.where(at == 2, low.astype(F32), 0.0)),
    )
    out_ref[TOK:ROWS, 0:TOK] = parts.astype(BF16)
    out_ref[TOK:ROWS, TOK:FEAT] = jnp.zeros((16, FEAT - TOK), BF16)


def first_kernel(info, latents_ref, scale_ref, table_ref, out_ref):
    modulate(info, 0, latents_ref[...], scale_ref, table_ref, out_ref)


def gather_parts(rows):
    third = (rows // 3 + 15) // 16 * 16
    return (0, third, 2 * third, rows)


def shard_ids(x, l, c):
    def index(dx, other):
        return lax.rem(x + dx, 4) * 4 + (1 - l if other else l) * 2

    rounds = [
        [index(0, False)],
        [index(3, False), index(1, False), index(0, True)],
        [index(2, False), index(1, True), index(3, True)],
        [index(2, True)],
    ]
    return [
        jnp.stack([v + c for v in r] + [v + 1 - c for v in r]).astype(jnp.int32) for r in rounds
    ]


def gather_rounds(shard, absorb):
    rows = shard.shape[0]
    cuts = gather_parts(rows)
    swap = functools.partial(move_t, pairs=C_SWAP)
    from_left, from_right = move_t(shard, X_UP), move_t(shard, X_DOWN)
    from_z = move_t(shard, Z_SWAP)
    absorb(0, [shard], [swap(shard)])
    first = [from_left, from_right, from_z]
    far = move_t(from_left, X_UP)
    right_z = move_t(from_z, X_DOWN)
    left_z = move_t(from_left, Z_SWAP)
    absorb(1, first, [swap(v) for v in first])
    second = [far, right_z, left_z]
    last = [
        move_t(far[cuts[0] : cuts[1]], Z_SWAP),
        move_t(left_z[cuts[1] : cuts[2]], X_UP),
        move_t(right_z[cuts[2] : cuts[3]], X_DOWN),
    ]
    absorb(2, second, [swap(v) for v in second])
    absorb(3, last, [swap(v) for v in last])


def shards_of(refs, count, parts, scratch, step):
    if not parts:
        return [(k, refs[k]) for k in range(count)]
    return [(k, scratch.at[k]) for k in range(count)]


def project_kernel(info_ids, *refs, count, parts, first, last):
    refs = list(refs)
    if not first:
        total_in, square_in = refs[0], refs[1]
        refs = refs[2:]
    given = refs[: count * (3 if parts else 1)]
    refs = refs[len(given) :]
    weight_ref = refs[0]
    refs = refs[1:]
    if last:
        outs, refs = refs[:4], refs[4:]
        total, square = refs[0], refs[1]
        refs = refs[2:]
    else:
        total, square = refs[0], refs[1]
        refs = refs[2:]
    step = pl.program_id(0)

    @pl.when(step == 0)
    def _():
        if first:
            total[...] = jnp.zeros_like(total)
            square[...] = jnp.zeros_like(square)
        else:
            total[...] = total_in[...]
            square[...] = square_in[...]
        if parts:
            whole = refs[0]
            cuts = gather_parts(ROWS)
            for k in range(count):
                for i in range(3):
                    whole[k, cuts[i] : cuts[i + 1], :] = given[3 * k + i][...]

    for k in range(count):

        @pl.when(step == k)
        def _(k=k):
            shard = refs[0].at[k] if parts else given[k]
            lhs = shard[0:TOK, :]
            for i in range(3):
                total[i] += jnp.dot(lhs, weight_ref[i], preferred_element_type=F32)
            piece = shard[TOK:ROWS, 0:TOK].astype(F32)
            square[...] += jnp.broadcast_to(jnp.sum(piece, axis=0, keepdims=True), square.shape)

    if last:

        @pl.when(step == count - 1)
        def _():
            rstd = lax.rsqrt(square[...] / D + 1e-06)
            rstd = jnp.transpose(jnp.broadcast_to(rstd[0:1, :], (128, TOK)))
            for i in range(3):
                for j in range(2):
                    at = slice(j * HD, (j + 1) * HD)
                    total[i, :, at] = total[i, :, at] * rstd
            z_hi = info_ids[count]
            for out, (a, b) in zip(outs, PIECES):
                j = lax.rem(z_hi + a, 2)
                s = lax.rem(z_hi // 2 + b, 2)
                rows = pl.ds(pl.multiple_of(s * HALF, HALF), HALF)
                cols = pl.ds(pl.multiple_of(j * HD, HD), HD)
                for i in range(3):
                    out[i] = total[i, rows, cols].astype(BF16)


def project(shard, weights, ids, z_hi):
    state = []

    def absorb(number, own, other):
        nonlocal state
        parts, first, last = number == 3, number == 0, number == 3
        given = own + other
        count = 2 if parts else len(given)
        kernel = functools.partial(project_kernel, count=count, parts=parts, first=first, last=last)
        totals = [sds((3, TOK, COLS), F32), sds((8, TOK), F32)]
        if last:
            out_shape = [sds((3, HALF, HD), BF16)] * 4
            scratch = [pltpu.VMEM(v.shape, F32) for v in totals]
        else:
            out_shape, scratch = totals, []
        if parts:
            scratch.append(pltpu.VMEM((count, ROWS, FEAT), BF16))
        state = call(
            kernel,
            out_shape,
            [VM] * (len(state) + len(given))
            + [pl.BlockSpec((3, FEAT, COLS), lambda i, ids: (0, ids[i], 0))],
            [VM] * len(out_shape),
            grid=(count,),
            scratch=scratch,
            flops=2 * count * TOK * FEAT * 768,
            size=count * 3 * FEAT * COLS * 2,
        )(jnp.concatenate([ids[number], z_hi[None]]), *state, *given, weights)

    gather_rounds(shard, absorb)
    return state


def attend_kernel(info, *refs, count, first, last):
    refs = list(refs)
    queries = refs[:4]
    bias = refs[4]
    blocks = refs[5 : 5 + 2 * count]
    refs = refs[5 + 2 * count :]
    if not first:
        top_in, sum_in, total_in = refs[:3]
        refs = refs[3:]
    if last:
        out = refs[0]
        top, summed, total = refs[1:4]
        refs = refs[4:]
    else:
        top, summed, total = refs[:3]
        refs = refs[3:]
    scores = refs[0]
    if first:
        top[...] = jnp.full_like(top, NEG)
        summed[...] = jnp.zeros_like(summed)
        total[...] = jnp.zeros_like(total)
    else:
        top[...] = top_in[...]
        summed[...] = sum_in[...]
        total[...] = total_in[...]
    scale = math.log2(math.e) / math.sqrt(HD)
    for p in range(4):
        rows = slice(p * HALF, (p + 1) * HALF)
        query = queries[p][0]
        old = top[rows, :]
        best = old[:, 0:1]
        for k in range(count):
            key = blocks[2 * k][...].reshape(4 * HALF, HD)
            score = lax.dot_general(query, key, (((1,), (1,)), ((), ())), preferred_element_type=F32)
            score = score * scale + bias[p, k][None, :]
            scores[k] = score
            best = jnp.maximum(best, jnp.max(score, axis=1, keepdims=True))
        shrink = jnp.exp2(old - best)
        weight_sum = jnp.zeros((HALF, 1), F32)
        acc = total[rows, :] * shrink
        for k in range(count):
            weight = jnp.exp2(scores[k] - best)
            weight_sum += jnp.sum(weight, axis=1, keepdims=True)
            value = blocks[2 * k + 1][...].reshape(4 * HALF, HD)
            acc += jnp.dot(weight.astype(BF16), value, preferred_element_type=F32)
        new_sum = summed[rows, :] * shrink + weight_sum
        if last:
            out[p] = (acc / new_sum).astype(BF16)
        else:
            top[rows, :] = jnp.broadcast_to(best, (HALF, HD))
            summed[rows, :] = new_sum
            total[rows, :] = acc


def attend(queries, bias, blocks, state, info, last):
    count = len(blocks)
    first = not state
    kernel = functools.partial(attend_kernel, count=count, first=first, last=last)
    carried = [sds((4 * HALF, HD), F32)] * 3
    scratch = [pltpu.VMEM((count, HALF, 4 * HALF), F32)]
    if last:
        out_shape = [sds((4, HALF, HD), BF16)]
        scratch = [pltpu.VMEM(v.shape, F32) for v in carried] + scratch
    else:
        out_shape = carried
    flat = [v for pair in blocks for v in pair]
    return call(
        kernel,
        out_shape,
        [VM] * (5 + len(flat) + len(state)),
        [VM] * len(out_shape),
        scratch=scratch,
        limit=24,
        flops=4 * 512 * 512 * count * HD * 2,
        size=MB,
    )(info, *queries, bias, *flat, *state)


def assemble_kernel(info, *refs):
    out = refs[4]
    z_hi = info[4]
    for piece, (a, b) in zip(refs[:4], PIECES):
        j = lax.rem(z_hi + a, 2)
        s = lax.rem(z_hi // 2 + b, 2)
        rows = pl.ds(pl.multiple_of(s * HALF, HALF), HALF)
        cols = pl.ds(pl.multiple_of(j * HD, HD), HD)
        out[rows, cols] = piece[...]


def output_kernel(info, *refs, count, parts, first, last, step):
    refs = list(refs)
    if not first:
        total_in = refs[0]
        refs = refs[1:]
    given = refs[: count * (3 if parts else 1)]
    refs = refs[len(given) :]
    weight_ref = refs[0]
    refs = refs[1:]
    if last:
        den_ref, sizes_ref, scale_ref, table_ref = refs[:4]
        outs = refs[4:6]
        total, whole = refs[6:8]
    else:
        total = refs[0]
    at = pl.program_id(0)

    @pl.when(at == 0)
    def _():
        if first:
            total[...] = jnp.zeros_like(total)
        else:
            total[...] = total_in[...]
        if parts:
            cuts = gather_parts(TOK)
            for k in range(count):
                for i in range(3):
                    whole[k, cuts[i] : cuts[i + 1], :] = given[3 * k + i][...]

    for k in range(count):

        @pl.when(at == k)
        def _(k=k):
            shard = whole.at[k] if parts else given[k]
            total[...] += jnp.dot(shard[...], weight_ref[...], preferred_element_type=F32)

    if last:

        @pl.when(at == count - 1)
        def _():
            velocity = total[...]
            scalars = info.at[pl.ds(count, 8)]
            size = sizes_ref[scalars[5 + step]]
            denoised = den_ref[...] + size * velocity
            outs[0][...] = denoised
            if step == STEPS - 1:
                outs[1][...] = velocity.astype(BF16)
            else:
                modulate(scalars, step + 1, denoised, scale_ref, table_ref, outs[1])


def output(attended, weights, ids, info, denoised, sizes, scales, table, step):
    state = []

    def absorb(number, own, other):
        nonlocal state
        parts, first, last = number == 3, number == 0, number == 3
        given = own + other
        count = 2 if parts else len(given)
        kernel = functools.partial(
            output_kernel, count=count, parts=parts, first=first, last=last, step=step
        )
        out_shape, scratch, extra, specs = [sds((TOK, FEAT), F32)], [], [], []
        if last:
            scratch = [pltpu.VMEM((TOK, FEAT), F32), pltpu.VMEM((count, TOK, COLS), BF16)]
            tail = sds((TOK, FEAT), BF16) if step == STEPS - 1 else sds((ROWS, FEAT), BF16)
            out_shape = out_shape + [tail]
            extra = [denoised, sizes, scales, table]
            specs = [VM, SM, VM, VM]
        state = call(
            kernel,
            out_shape,
            [VM] * (len(state) + len(given))
            + [pl.BlockSpec((COLS, FEAT), lambda i, ids: (ids[i], 0))]
            + specs,
            [VM] * len(out_shape),
            grid=(count,),
            scratch=scratch,
            flops=2 * count * TOK * FEAT * COLS,
            size=count * FEAT * COLS * 2,
        )(jnp.concatenate([ids[number], info]), *state, *given, weights, *extra)

    gather_rounds(attended, absorb)
    return state


def body(
    latents,
    input_weights,
    output_weights,
    position_table,
    level_scale,
    step_sizes,
    levels,
    group_order,
    group_mask,
):
    t = lax.axis_index("tensor")
    g = lax.axis_index("group")
    x, l, c = t // 4, t // 2 % 2, t % 2
    y, z = g // 4, g % 4
    info = jnp.stack([x, l, c, y, z, levels[0, 0], levels[0, 1], group_order[0]]).astype(jnp.int32)
    ids = shard_ids(x, l, c)

    mask_rows = jnp.concatenate(
        [lax.ppermute(group_mask, BOTH, pairs) for pairs in HEAD_PERMS], axis=0
    )
    source = [
        jnp.stack([2 * ((core + b) % 2) + (z + a) % 2 for a, b in PIECES]) for core in (c, 1 - c)
    ]
    order = (0, 3, 1, 2)
    columns = jnp.concatenate([(y + dy) % 4 * 4 + s for dy in order for s in source])
    bias = jnp.where(jnp.take(mask_rows, columns, axis=1) > 0, 0.0, NEG).astype(F32)
    bias = jnp.repeat(bias, HALF, axis=1).reshape(4, 8, 4 * HALF)

    shard = call(first_kernel, [sds((ROWS, FEAT), BF16)], [VM] * 3, [VM])(
        info, latents, level_scale, position_table
    )[0]
    denoised = latents
    for step in range(STEPS):
        pieces = project(shard, input_weights, ids, z)
        pieces = [lax.ppermute(v, BOTH, pairs) for v, pairs in zip(pieces, HEAD_PERMS)]
        swap = functools.partial(move_t, pairs=C_SWAP)
        near = jnp.stack([v[1:] for v in pieces], axis=1)
        below, above = move_g(near, Y_UP), move_g(near, Y_DOWN)
        near_other = swap(near)
        far_keys = move_g(below[0], Y_UP)
        far_values = move_g(above[1], Y_DOWN)
        below_other, above_other = swap(below), swap(above)
        far_keys_other, far_values_other = swap(far_keys), swap(far_values)
        pair = lambda v: (v[0], v[1])
        state = attend(pieces, bias[:, 0:2], [pair(near), pair(near_other)], [], info, False)
        state = attend(
            pieces,
            bias[:, 2:6],
            [pair(below), pair(below_other), pair(above), pair(above_other)],
            state,
            info,
            False,
        )
        attended = attend(
            pieces,
            bias[:, 6:8],
            [(far_keys, far_values), (far_keys_other, far_values_other)],
            state,
            info,
            True,
        )[0]
        back = [lax.ppermute(attended[p], BOTH, BACK_PERMS[p]) for p in range(4)]
        attended = call(assemble_kernel, [sds((TOK, COLS), BF16)], [VM] * 4, [VM])(info, *back)[0]
        denoised, shard = output(
            attended, output_weights, ids, info, denoised, step_sizes, level_scale, position_table, step
        )
    return (denoised, shard)


def solution(mesh):
    placed = (
        P("group", "tensor"),
        P(None, None, "tensor"),
        P(None, "tensor"),
        P(None, "tensor"),
        P(None, "tensor"),
        P(),
        P("group", None),
        P("group"),
        P("group", None),
    )
    return jax.shard_map(
        body,
        mesh=mesh,
        in_specs=placed,
        out_specs=(P("group", "tensor"), P("group", "tensor")),
        check_vma=False,
    )
```

```python
import functools
import math

import jax
import jax.numpy as jnp
from jax import lax
from jax.experimental import pallas as pl
from jax.experimental.pallas import tpu as pltpu
from jax.sharding import PartitionSpec as P


D = 6144
HD = 128
STEPS = 2
HALF = 128
FEAT = 384
CHIP = 2 * FEAT
COLS = 256
CHIP_COLS = 2 * COLS
ROWS = HALF + 16
NEG = -1e30
F32 = jnp.float32
BF16 = jnp.bfloat16
VM = pl.BlockSpec(memory_space=pltpu.VMEM)
SM = pl.BlockSpec(memory_space=pltpu.SMEM)
MB = 1 << 20
BOTH = ("group", "tensor")


def t_perm(move):
    pairs = []
    for t in range(16):
        x, l, c = move(t // 4, t // 2 % 2, t % 2)
        pairs.append((t, (x % 4) * 4 + l * 2 + c))
    return pairs


def g_perm(dy, dz):
    return [(g, (g // 4 + dy) % 4 * 4 + (g + dz) % 4) for g in range(16)]


X_UP = t_perm(lambda x, l, c: (x + 1, l, c))
X_DOWN = t_perm(lambda x, l, c: (x - 1, l, c))
X_FAR = t_perm(lambda x, l, c: (x + 2, l, c))
Z_SWAP = t_perm(lambda x, l, c: (x, 1 - l, c))
C_SWAP = t_perm(lambda x, l, c: (x, l, 1 - c))
Y_UP, Y_DOWN, Y_FAR = g_perm(1, 0), g_perm(-1, 0), g_perm(2, 0)
Z_MOVES = {1: g_perm(0, 1), 2: g_perm(0, 2), 3: g_perm(0, -1)}


def move_t(array, pairs):
    return lax.ppermute(array, "tensor", pairs)


def move_g(array, pairs):
    return lax.ppermute(array, "group", pairs)


def swap(array):
    return lax.ppermute(array, "tensor", C_SWAP)


def sds(shape, dtype):
    return jax.ShapeDtypeStruct(shape, dtype)


def call(kernel, out_shape, in_specs, out_specs, scratch=(), limit=12, flops=0, size=0):
    return pl.pallas_call(
        kernel,
        out_shape=out_shape,
        in_specs=in_specs,
        out_specs=out_specs,
        scratch_shapes=scratch,
        compiler_params=pltpu.CompilerParams(vmem_limit_bytes=limit * MB),
        cost_estimate=pl.CostEstimate(flops=flops, bytes_accessed=size, transcendentals=0),
    )


def place():
    t, g = lax.axis_index("tensor"), lax.axis_index("group")
    return t // 4, t // 2 % 2, t % 2, g // 4, g % 4


def modulated(shifted_from, level, order, scale_ref, table_ref):
    table = table_ref[...].astype(F32)
    row_at = lax.broadcasted_iota(jnp.int32, table.shape, 0)
    position = jnp.sum(jnp.where(row_at == order, table, 0.0), axis=0, keepdims=True)
    shifted = shifted_from + position
    factor = 1.0 + scale_ref[pl.ds(level, 1), :]
    squares = jnp.sum(shifted * shifted, axis=1, keepdims=True)
    lanes = jnp.transpose(jnp.broadcast_to(squares, (HALF, HALF)))[0:16, :]
    high = lanes.astype(BF16).astype(F32)
    middle = (lanes - high).astype(BF16).astype(F32)
    low = lanes - high - middle
    at = lax.broadcasted_iota(jnp.int32, lanes.shape, 0)
    parts = jnp.where(at == 0, high, jnp.where(at == 1, middle, jnp.where(at == 2, low, 0.0)))
    return (shifted * factor).astype(BF16), parts.astype(BF16)


def store_modulated(out, features, parts):
    out[0:HALF, :] = features
    out[HALF:ROWS, 0:HALF] = parts
    out[HALF:ROWS, HALF:FEAT] = jnp.zeros((16, FEAT - HALF), BF16)


def first_kernel(levels, order, latents, scale, table, keep, send, keep_latents, send_latents):
    core = place()[2]
    for half, out, out_latents in ((core, keep, keep_latents), (1 - core, send, send_latents)):
        rows = latents[pl.ds(pl.multiple_of(half * HALF, HALF), HALF), :]
        out_latents[...] = rows
        store_modulated(out, *modulated(rows, levels[0, 0], order[0], scale, table))


def pair_kernel(own, other, out):
    core = place()[2]
    out[core] = own[...]
    out[1 - core] = other[...]


def gather_rounds(shard):
    z = move_t(shard, Z_SWAP)
    far = move_t(shard, X_FAR)
    left, right = move_t(shard, X_UP), move_t(shard, X_DOWN)
    z_left, z_right = move_t(z, X_UP), move_t(z, X_DOWN)
    z_far = move_t(far, Z_SWAP)
    return [
        [(0, False, shard), (0, True, z), (3, False, left), (1, False, right)],
        [(2, False, far), (3, True, z_left), (1, True, z_right)],
        [(2, True, z_far)],
    ]


def chip_of(x, l, dx, other):
    return lax.rem(x + dx, 4) * 2 + (1 - l if other else l)


def project_kernel(*refs, shards, first, last):
    refs = list(refs)
    total_in = square_in = None
    if not first:
        total_in, square_in = refs[:2]
        refs = refs[2:]
    given = refs[: len(shards)]
    weights = refs[len(shards) : len(shards) + 2]
    outs = refs[len(shards) + 2 :]
    x, l, core, _, z = place()
    lhs, starts = [], []
    square = jnp.zeros((8, HALF), F32) if first else square_in[...]
    for (dx, other), shard in zip(shards, given):
        lhs.append(jnp.concatenate([shard[0, 0:HALF, :], shard[1, 0:HALF, :]], axis=1))
        starts.append(pl.multiple_of(chip_of(x, l, dx, other) * CHIP, CHIP))
        for f in range(2):
            rows = jnp.sum(shard[f, HALF:ROWS, 0:HALF].astype(F32), axis=0, keepdims=True)
            square = square + jnp.broadcast_to(rows, square.shape)
    if last:
        total = outs[4]
        rstd = lax.rsqrt(square[0:1, :] / D + 1e-06)
        rstd = jnp.transpose(jnp.broadcast_to(rstd, (HALF, HALF)))
        rstd = jnp.concatenate([rstd, rstd], axis=1)
    else:
        total = outs[0]
        outs[1][...] = square
    for s in range(2):
        for i in range(3):
            acc = None if first else total_in[s, i]
            for row, start in zip(lhs, starts):
                part = jnp.dot(row, weights[s][i, pl.ds(start, CHIP), :], preferred_element_type=F32)
                acc = part if acc is None else acc + part
            if last:
                acc = acc * rstd
                if i == 0:
                    acc = acc * (math.log2(math.e) / math.sqrt(HD))
            total[s, i] = acc
    if last:
        for j in range(4):
            head = lax.rem(z + j, 4)
            which = jnp.where(head // 2 == core, 0, 1)
            cols = pl.ds(pl.multiple_of(lax.rem(head, 2) * HD, HD), HD)
            for i in range(3):
                outs[j][i] = total[which, i, :, cols].astype(BF16)


def project(shard, weights):
    state = []
    rounds = gather_rounds(shard)
    for number, given in enumerate(rounds):
        first, last = number == 0, number == len(rounds) - 1
        shards = [(dx, other) for dx, other, _ in given]
        totals = [sds((2, 3, HALF, COLS), F32), sds((8, HALF), F32)]
        out_shape = [sds((3, HALF, HD), BF16)] * 4 if last else totals
        state = call(
            functools.partial(project_kernel, shards=shards, first=first, last=last),
            out_shape,
            [VM] * (len(state) + len(given) + 2),
            [VM] * len(out_shape),
            scratch=[pltpu.VMEM(totals[0].shape, F32)] if last else [],
            flops=2 * len(given) * HALF * CHIP * 6 * COLS,
            size=len(given) * CHIP * 6 * COLS * 2,
        )(*state, *[v for _, _, v in given], *weights)
    return state


def attend_kernel(*refs, offsets, first, last):
    refs = list(refs)
    masks, queries = refs[:4], refs[4:8]
    count = len(offsets)
    blocks = refs[8 : 8 + count]
    refs = refs[8 + count :]
    if not first:
        top_in, sum_in, total_in = refs[:3]
        refs = refs[3:]
    outs, scores = refs[:-1], refs[-1]
    _, _, _, y, z = place()
    query = jnp.concatenate([q[0] for q in queries], axis=0)
    best = jnp.full((4 * HALF, 1), NEG, F32) if first else top_in[...][:, 0:1]
    for k, (dy, block) in enumerate(zip(offsets, blocks)):
        keys = block[0].reshape(4 * HALF, HD)
        score = lax.dot_general(query, keys, (((1,), (1,)), ((), ())), preferred_element_type=F32)
        rows = []
        for p in range(4):
            bias = [
                jnp.where(masks[p][0, lax.rem(y + dy, 4) * 4 + lax.rem(z + j, 4)] > 0, 0.0, NEG)
                for j in range(4)
            ]
            rows.append(
                jnp.concatenate(
                    [
                        score[p * HALF : (p + 1) * HALF, j * HALF : (j + 1) * HALF] + bias[j]
                        for j in range(4)
                    ],
                    axis=1,
                )
            )
        score = jnp.concatenate(rows, axis=0)
        scores[k] = score
        best = jnp.maximum(best, jnp.max(score, axis=1, keepdims=True))
    summed = jnp.zeros((4 * HALF, 1), F32)
    acc = jnp.zeros((4 * HALF, HD), F32)
    if not first:
        shrink = jnp.exp2(top_in[...] - best)
        summed = (sum_in[...] * shrink)[:, 0:1]
        acc = total_in[...] * shrink
    for k, block in enumerate(blocks):
        weight = jnp.exp2(scores[k] - best)
        summed = summed + jnp.sum(weight, axis=1, keepdims=True)
        values = block[1].reshape(4 * HALF, HD)
        acc = acc + jnp.dot(weight.astype(BF16), values, preferred_element_type=F32)
    if last:
        result = (acc / summed).astype(BF16)
        for p in range(4):
            outs[p][...] = result[p * HALF : (p + 1) * HALF, :]
    else:
        outs[0][...] = jnp.broadcast_to(best, (4 * HALF, HD))
        outs[1][...] = jnp.broadcast_to(summed, (4 * HALF, HD))
        outs[2][...] = acc


def attend(masks, queries, blocks, state, last):
    offsets = [dy for dy, _ in blocks]
    out_shape = [sds((HALF, HD), BF16)] * 4 if last else [sds((4 * HALF, HD), F32)] * 3
    return call(
        functools.partial(attend_kernel, offsets=offsets, first=not state, last=last),
        out_shape,
        [SM] * 4 + [VM] * (4 + len(blocks) + len(state)),
        [VM] * len(out_shape),
        scratch=[pltpu.VMEM((len(blocks), 4 * HALF, 4 * HALF), F32)],
        limit=16,
        flops=4 * 512 * 512 * len(blocks) * HD * 4,
        size=MB,
    )(*masks, *queries, *[v for _, v in blocks], *state)


def output_kernel(*refs, shards, first, last, step):
    refs = list(refs)
    if not first:
        total_in = refs[0]
        refs = refs[1:]
    given = refs[: len(shards)]
    weights = refs[len(shards) : len(shards) + 2]
    refs = refs[len(shards) + 2 :]
    if last:
        levels, order, sizes = refs[:3]
        dens, scales, tables = refs[3:5], refs[5:7], refs[7:9]
        outs = refs[9:-1]
    else:
        outs = refs[:-1]
    heads = refs[-1]
    x, l, core, _, z = place()
    starts = []
    for n, ((dx, other), shard) in enumerate(zip(shards, given)):
        starts.append(pl.multiple_of(chip_of(x, l, dx, other) * CHIP_COLS, CHIP_COLS))
        for j in range(4):
            cols = pl.ds(pl.multiple_of(lax.rem(z + j, 4) * HD, HD), HD)
            heads[n, :, cols] = shard[j]
    for s in range(2):
        acc = None if first else total_in[s]
        for n, start in enumerate(starts):
            part = jnp.dot(
                heads[n], weights[s][pl.ds(start, CHIP_COLS), :], preferred_element_type=F32
            )
            acc = part if acc is None else acc + part
        if not last:
            outs[0][s] = acc
            continue
        denoised = dens[s][...] + sizes[levels[0, step]] * acc
        outs[s][...] = denoised
        if step == STEPS - 1:
            outs[2 + s][...] = acc.astype(BF16)
        else:
            f = core if s == 0 else 1 - core
            store_modulated(
                outs[2].at[f],
                *modulated(denoised, levels[0, step + 1], order[0], scales[s], tables[s]),
            )


def output(attended, weights, step, levels, order, sizes, dens, scales, tables):
    state = []
    rounds = gather_rounds(attended)
    for number, given in enumerate(rounds):
        first, last = number == 0, number == len(rounds) - 1
        shards = [(dx, other) for dx, other, _ in given]
        out_shape, extra, specs = [sds((2, HALF, FEAT), F32)], [], []
        if last:
            out_shape = [sds((HALF, FEAT), F32)] * 2
            if step == STEPS - 1:
                out_shape = out_shape + [sds((HALF, FEAT), BF16)] * 2
            else:
                out_shape = out_shape + [sds((2, ROWS, FEAT), BF16)]
            extra = [levels, order, sizes, *dens, *scales, *tables]
            specs = [SM] * 3 + [VM] * 6
        state = call(
            functools.partial(output_kernel, shards=shards, first=first, last=last, step=step),
            out_shape,
            [VM] * (len(state) + len(given) + 2) + specs,
            [VM] * len(out_shape),
            scratch=[pltpu.VMEM((len(given), HALF, CHIP_COLS), BF16)],
            flops=2 * len(given) * HALF * CHIP_COLS * CHIP,
            size=len(given) * CHIP_COLS * CHIP * 2,
        )(*state, *[v for _, _, v in given], *weights, *extra)
    return state


def join_kernel(own_a, other_a, own_b, other_b, out_a, out_b):
    core = place()[2]
    for own, other, out in ((own_a, other_a, out_a), (own_b, other_b, out_b)):
        out[pl.ds(pl.multiple_of(core * HALF, HALF), HALF), :] = own[...]
        out[pl.ds(pl.multiple_of((1 - core) * HALF, HALF), HALF), :] = other[...]


def body(
    latents,
    input_weights,
    output_weights,
    position_table,
    level_scale,
    step_sizes,
    levels,
    group_order,
    group_mask,
):
    keep, send, keep_latents, send_latents = call(
        first_kernel,
        [sds((ROWS, FEAT), BF16)] * 2 + [sds((HALF, FEAT), F32)] * 2,
        [SM] * 2 + [VM] * 3,
        [VM] * 4,
    )(levels, group_order, latents, level_scale, position_table)
    shard = call(pair_kernel, sds((2, ROWS, FEAT), BF16), [VM] * 2, VM)(keep, swap(send))
    in_weights = [input_weights, swap(input_weights)]
    out_weights = [output_weights, swap(output_weights)]
    scales = [level_scale, swap(level_scale)]
    tables = [position_table, swap(position_table)]
    dens = [keep_latents, swap(send_latents)]
    masks = [group_mask] + [move_g(group_mask, Z_MOVES[4 - j]) for j in (1, 2, 3)]

    for step in range(STEPS):
        sent = project(shard, in_weights)
        pieces = [sent[0]] + [move_g(sent[4 - j], Z_MOVES[4 - j]) for j in (1, 2, 3)]
        near = jnp.stack([v[1:] for v in pieces], axis=1)
        far = move_g(near, Y_FAR)
        below, above = move_g(near, Y_UP), move_g(near, Y_DOWN)
        state = attend(masks, pieces, [(0, near), (0, swap(near))], [], False)
        state = attend(
            masks,
            pieces,
            [(3, below), (3, swap(below)), (1, above), (1, swap(above))],
            state,
            False,
        )
        attended = attend(masks, pieces, [(2, far), (2, swap(far))], state, True)
        attended = [attended[0]] + [move_g(attended[4 - j], Z_MOVES[4 - j]) for j in (1, 2, 3)]
        result = output(
            jnp.stack(attended),
            out_weights,
            step,
            levels,
            group_order,
            step_sizes,
            dens,
            scales,
            tables,
        )
        dens = result[:2]
        shard = result[2]
    return tuple(
        call(
            join_kernel,
            [sds((2 * HALF, FEAT), F32), sds((2 * HALF, FEAT), BF16)],
            [VM] * 4,
            [VM] * 2,
        )(result[0], swap(result[1]), result[2], swap(result[3]))
    )


def solution(mesh):
    placed = (
        P("group", "tensor"),
        P(None, None, "tensor"),
        P(None, "tensor"),
        P(None, "tensor"),
        P(None, "tensor"),
        P(),
        P("group", None),
        P("group"),
        P("group", None),
    )
    return jax.shard_map(
        body,
        mesh=mesh,
        in_specs=placed,
        out_specs=(P("group", "tensor"), P("group", "tensor")),
        check_vma=False,
    )
```

```python
import functools
import math

import jax
import jax.numpy as jnp
from jax import lax
from jax.experimental import pallas as pl
from jax.experimental.pallas import tpu as pltpu
from jax.sharding import PartitionSpec as P


D = 6144
HD = 128
STEPS = 2
HALF = 128
FEAT = 384
CHIP = 2 * FEAT
COLS = 256
CHIP_COLS = 2 * COLS
ROWS = HALF + 16
PIECE = 3 * HALF + 16
NEG = -1e30
F32 = jnp.float32
BF16 = jnp.bfloat16
VM = pl.BlockSpec(memory_space=pltpu.VMEM)
HBM = pl.BlockSpec(memory_space=pltpu.HBM)
SM = pl.BlockSpec(memory_space=pltpu.SMEM)
MB = 1 << 20
QUERIES = 4 * HALF
CHUNK = 256
BOTH = ("group", "tensor")


def t_perm(move):
    pairs = []
    for t in range(16):
        x, l, c = move(t // 4, t // 2 % 2, t % 2)
        pairs.append((t, (x % 4) * 4 + l * 2 + c))
    return pairs


def g_perm(dy, dz):
    return [(g, (g // 4 + dy) % 4 * 4 + (g + dz) % 4) for g in range(16)]


X_UP = t_perm(lambda x, l, c: (x + 1, l, c))
X_DOWN = t_perm(lambda x, l, c: (x - 1, l, c))
X_FAR = t_perm(lambda x, l, c: (x + 2, l, c))
Z_SWAP = t_perm(lambda x, l, c: (x, 1 - l, c))
C_SWAP = t_perm(lambda x, l, c: (x, l, 1 - c))
Y_UP, Y_DOWN, Y_FAR = g_perm(1, 0), g_perm(-1, 0), g_perm(2, 0)
Z_MOVES = {1: g_perm(0, 1), 2: g_perm(0, 2), 3: g_perm(0, -1)}


def move_t(array, pairs):
    return lax.ppermute(array, "tensor", pairs)


def move_g(array, pairs):
    return lax.ppermute(array, "group", pairs)


def swap(array):
    return lax.ppermute(array, "tensor", C_SWAP)


def after(array, *others):
    return lax.optimization_barrier((array, *others))[0]


def sds(shape, dtype):
    return jax.ShapeDtypeStruct(shape, dtype)


def call(kernel, out_shape, in_specs, out_specs, scratch=(), limit=12, flops=0, size=0):
    return pl.pallas_call(
        kernel,
        out_shape=out_shape,
        in_specs=in_specs,
        out_specs=out_specs,
        scratch_shapes=scratch,
        compiler_params=pltpu.CompilerParams(vmem_limit_bytes=limit * MB),
        cost_estimate=pl.CostEstimate(flops=flops, bytes_accessed=size, transcendentals=0),
    )


def place():
    t, g = lax.axis_index("tensor"), lax.axis_index("group")
    return t // 4, t // 2 % 2, t % 2, g // 4, g % 4


def modulated(shifted_from, level, order, scale_ref, table_ref):
    table = table_ref[...].astype(F32)
    row_at = lax.broadcasted_iota(jnp.int32, table.shape, 0)
    position = jnp.sum(jnp.where(row_at == order, table, 0.0), axis=0, keepdims=True)
    shifted = shifted_from + position
    factor = 1.0 + scale_ref[pl.ds(level, 1), :]
    squares = jnp.sum(shifted * shifted, axis=1, keepdims=True)
    lanes = jnp.transpose(jnp.broadcast_to(squares, (HALF, HALF)))[0:16, :]
    high = lanes.astype(BF16).astype(F32)
    middle = (lanes - high).astype(BF16).astype(F32)
    low = lanes - high - middle
    at = lax.broadcasted_iota(jnp.int32, lanes.shape, 0)
    parts = jnp.where(at == 0, high, jnp.where(at == 1, middle, jnp.where(at == 2, low, 0.0)))
    return (shifted * factor).astype(BF16), parts.astype(BF16)


def store_modulated(out, features, parts):
    out[0:HALF, :] = features
    out[HALF:ROWS, 0:HALF] = parts
    out[HALF:ROWS, HALF:FEAT] = jnp.zeros((16, FEAT - HALF), BF16)


def first_kernel(*refs):
    sources, outs, held, sems = refs[:5], refs[5:9], refs[9:14], refs[14]
    copies = [
        pltpu.make_async_copy(source, target, sems.at[i])
        for i, (source, target) in enumerate(zip(sources, held))
    ]
    for copy in copies:
        copy.start()
    for copy in copies:
        copy.wait()
    levels, order, latents, scale, table = held
    keep, send, keep_latents, send_latents = outs
    core = place()[2]
    for half, out, out_latents in ((core, keep, keep_latents), (1 - core, send, send_latents)):
        rows = latents[pl.ds(pl.multiple_of(half * HALF, HALF), HALF), :]
        out_latents[...] = rows
        store_modulated(out, *modulated(rows, levels[0, 0], order[0], scale, table))


def pair_kernel(own, other, weights, out):
    core = place()[2]
    out[core] = own[...]
    out[1 - core] = other[...]


def gather_rounds(shard):
    z = move_t(shard, Z_SWAP)
    far = move_t(shard, X_FAR)
    left, right = move_t(shard, X_UP), move_t(shard, X_DOWN)
    z_left, z_right = move_t(z, X_UP), move_t(z, X_DOWN)
    z_far = move_t(far, Z_SWAP)
    return [
        [(0, False, shard), (0, True, z), (3, False, left), (1, False, right)],
        [(2, False, far), (3, True, z_left), (1, True, z_right)],
        [(2, True, z_far)],
    ]


def chip_of(x, l, dx, other):
    return lax.rem(x + dx, 4) * 2 + (1 - l if other else l)


def project_kernel(*refs, shards, first, last):
    refs = list(refs)
    total_in = square_in = None
    if not first:
        total_in, square_in = refs[:2]
        refs = refs[2:]
    given = refs[: len(shards)]
    weights = refs[len(shards) : len(shards) + 2]
    outs = refs[len(shards) + 2 :]
    if last:
        mask_ref, outs = outs[0], outs[1:]
    x, l, core, _, z = place()
    lhs, starts = [], []
    square = jnp.zeros((8, HALF), F32) if first else square_in[...]
    for (dx, other), shard in zip(shards, given):
        lhs.append(jnp.concatenate([shard[0, 0:HALF, :], shard[1, 0:HALF, :]], axis=1))
        starts.append(pl.multiple_of(chip_of(x, l, dx, other) * CHIP, CHIP))
        for f in range(2):
            rows = jnp.sum(shard[f, HALF:ROWS, 0:HALF].astype(F32), axis=0, keepdims=True)
            square = square + jnp.broadcast_to(rows, square.shape)
    if last:
        total = outs[4]
        rstd = lax.rsqrt(square[0:1, :] / D + 1e-06)
        rstd = jnp.transpose(jnp.broadcast_to(rstd, (HALF, HALF)))
        rstd = jnp.concatenate([rstd, rstd], axis=1)
    else:
        total = outs[0]
        outs[1][...] = square
    for s in range(2):
        for i in range(3):
            acc = None if first else total_in[s, i]
            for row, start in zip(lhs, starts):
                part = jnp.dot(row, weights[s][i, pl.ds(start, CHIP), :], preferred_element_type=F32)
                acc = part if acc is None else acc + part
            if last:
                acc = acc * rstd
                if i == 0:
                    acc = acc * (math.log2(math.e) / math.sqrt(HD))
            total[s, i] = acc
    if last:
        for j in range(4):
            head = lax.rem(z + j, 4)
            which = jnp.where(head // 2 == core, 0, 1)
            cols = pl.ds(pl.multiple_of(lax.rem(head, 2) * HD, HD), HD)
            for i in range(3):
                outs[j][i * HALF : (i + 1) * HALF, :] = total[which, i, :, cols].astype(BF16)
            mask = (mask_ref[...] > 0).astype(F32)
            outs[j][3 * HALF : PIECE, :] = jnp.zeros((16, HD), BF16)
            outs[j][3 * HALF : PIECE, 0:16] = jnp.broadcast_to(mask, (16, 16)).astype(BF16)


def project(shard, weights, group_mask):
    state = []
    rounds = gather_rounds(shard)
    for number, given in enumerate(rounds):
        first, last = number == 0, number == len(rounds) - 1
        shards = [(dx, other) for dx, other, _ in given]
        totals = [sds((2, 3, HALF, COLS), F32), sds((8, HALF), F32)]
        out_shape = [sds((PIECE, HD), BF16)] * 4 if last else totals
        extra = [group_mask] if last else []
        state = call(
            functools.partial(project_kernel, shards=shards, first=first, last=last),
            out_shape,
            [VM] * (len(state) + len(given) + 2 + len(extra)),
            [VM] * len(out_shape),
            scratch=[pltpu.VMEM(totals[0].shape, F32)] if last else [],
            flops=2 * len(given) * HALF * CHIP * 6 * COLS,
            size=len(given) * CHIP * 6 * COLS * 2,
        )(*state, *[v for _, _, v in given], *weights, *extra)
    return state


def attend_kernel(*refs, offsets, first, last):
    refs = list(refs)
    pieces, other = refs[:4], refs[4]
    count = len(offsets)
    keys, values = refs[5 : 5 + count], refs[5 + count : 5 + 2 * count]
    refs = refs[5 + 2 * count :]
    if not first:
        top_in, sum_in, total_in = refs[:3]
        refs = refs[3:]
    _, _, _, y, z = place()
    masks = [piece[3 * HALF : 3 * HALF + 1, :].astype(F32) for piece in pieces]
    lane = lax.broadcasted_iota(jnp.int32, (1, HD), 1)
    masks = [
        jnp.broadcast_to(jnp.where(lane < 16, (1.0 - m) * NEG, 0.0), (HALF, HD)).astype(BF16)
        for m in masks
    ]
    group_at = lax.broadcasted_iota(jnp.int32, (QUERIES, HD), 1)
    key_at = lax.broadcasted_iota(jnp.int32, (QUERIES, HD), 0)
    wide = []
    for dy, key in zip(offsets, keys):
        group = lax.rem(y + dy, 4) * 4 + lax.rem(z + key_at // HALF, 4)
        spread = jnp.where(group_at == group, 1.0, 0.0).astype(BF16)
        wide.append(jnp.concatenate([key[...].reshape(QUERIES, HD), spread], axis=1))
    for r in range(2 * QUERIES // CHUNK):
        mine = r * CHUNK < QUERIES
        rows = slice(r * CHUNK, (r + 1) * CHUNK)
        p = r * CHUNK % QUERIES // HALF
        query = [pieces[p + i][0:HALF, :] if mine else other[p + i] for i in range(2)]
        query = [jnp.concatenate([query[i], masks[p + i]], axis=1) for i in range(2)]
        query = jnp.concatenate(query, axis=0)
        scores = [
            lax.dot_general(query, key, (((1,), (1,)), ((), ())), preferred_element_type=F32)
            for key in wide
        ]
        best = functools.reduce(
            jnp.maximum, [s[:, i * HD : (i + 1) * HD] for s in scores for i in range(4)]
        )
        best = jnp.max(best, axis=1, keepdims=True)
        if not first:
            old = top_in[rows, :]
            best = jnp.maximum(best, old[:, 0:1])
            shrink = jnp.exp2(old - best)
            summed, acc = sum_in[rows, :] * shrink, total_in[rows, :] * shrink
        for k, score in enumerate(scores):
            weight = jnp.exp2(score - best)
            parts = sum(weight[:, i * HD : (i + 1) * HD] for i in range(4))
            part = jnp.dot(
                weight.astype(BF16),
                values[k][...].reshape(QUERIES, HD),
                preferred_element_type=F32,
            )
            if first and k == 0:
                summed, acc = parts, part
            else:
                summed, acc = summed + parts, acc + part
        if not last:
            refs[0][rows, :] = jnp.broadcast_to(best, (CHUNK, HD))
            refs[1][rows, :] = summed
            refs[2][rows, :] = acc
            continue
        summed = jnp.sum(summed, axis=1, keepdims=True)
        result = acc / summed
        level = best + jnp.log2(summed)
        rows = slice(r * CHUNK % QUERIES, r * CHUNK % QUERIES + CHUNK)
        out = refs[0] if mine else refs[1]
        out[rows, :] = result
        for i in range(2):
            line = jnp.broadcast_to(level[i * HALF : (i + 1) * HALF, :], (HALF, HD))
            out[QUERIES + p + i : QUERIES + p + i + 1, :] = jnp.transpose(line)[0:1, :]


def attend(pieces, other, blocks, state, last):
    offsets = [dy for dy, _, _ in blocks]
    out_shape = [sds((QUERIES + 8, HD), F32)] * 2 if last else [sds((2 * QUERIES, HD), F32)] * 3
    return call(
        functools.partial(attend_kernel, offsets=offsets, first=not state, last=last),
        out_shape,
        [VM] * (5 + 2 * len(blocks) + len(state)),
        [VM] * len(out_shape),
        limit=16,
        flops=4 * 1024 * 512 * len(blocks) * HD,
        size=MB,
    )(*pieces, other, *[k for _, k, _ in blocks], *[v for _, _, v in blocks], *state)


def merge_kernel(own, other, *outs):
    for p in range(4):
        rows = slice(p * HALF, (p + 1) * HALF)
        line = slice(QUERIES + p, QUERIES + p + 1)
        gap = jnp.transpose(jnp.broadcast_to(other[line, :] - own[line, :], (HALF, HD)))
        share = 1.0 / (1.0 + jnp.exp2(gap))
        outs[p][...] = (own[rows, :] * share + other[rows, :] * (1.0 - share)).astype(BF16)


def output_kernel(*refs, shards, first, last, step):
    refs = list(refs)
    if not first:
        total_in = refs[0]
        refs = refs[1:]
    given = refs[: len(shards)]
    weights = refs[len(shards) : len(shards) + 2]
    refs = refs[len(shards) + 2 :]
    if last:
        levels, order, sizes = refs[:3]
        dens, scales, tables = refs[3:5], refs[5:7], refs[7:9]
        outs = refs[9:-1]
    else:
        outs = refs[:-1]
    heads = refs[-1]
    x, l, core, _, z = place()
    starts = []
    for n, ((dx, other), shard) in enumerate(zip(shards, given)):
        starts.append(pl.multiple_of(chip_of(x, l, dx, other) * CHIP_COLS, CHIP_COLS))
        for j in range(4):
            cols = pl.ds(pl.multiple_of(lax.rem(z + j, 4) * HD, HD), HD)
            heads[n, :, cols] = shard[j]
    for s in range(2):
        acc = None if first else total_in[s]
        for n, start in enumerate(starts):
            part = jnp.dot(
                heads[n], weights[s][pl.ds(start, CHIP_COLS), :], preferred_element_type=F32
            )
            acc = part if acc is None else acc + part
        if not last:
            outs[0][s] = acc
            continue
        denoised = dens[s][...] + sizes[levels[0, step]] * acc
        outs[s][...] = denoised
        if step == STEPS - 1:
            outs[2 + s][...] = acc.astype(BF16)
        else:
            f = core if s == 0 else 1 - core
            store_modulated(
                outs[2].at[f],
                *modulated(denoised, levels[0, step + 1], order[0], scales[s], tables[s]),
            )


def output(attended, weights, step, levels, order, sizes, dens, scales, tables):
    state = []
    rounds = gather_rounds(attended)
    for number, given in enumerate(rounds):
        first, last = number == 0, number == len(rounds) - 1
        shards = [(dx, other) for dx, other, _ in given]
        out_shape, extra, specs = [sds((2, HALF, FEAT), F32)], [], []
        if last:
            out_shape = [sds((HALF, FEAT), F32)] * 2
            if step == STEPS - 1:
                out_shape = out_shape + [sds((HALF, FEAT), BF16)] * 2
            else:
                out_shape = out_shape + [sds((2, ROWS, FEAT), BF16)]
            extra = [levels, order, sizes, *dens, *scales, *tables]
            specs = [SM] * 3 + [VM] * 6
        state = call(
            functools.partial(output_kernel, shards=shards, first=first, last=last, step=step),
            out_shape,
            [VM] * (len(state) + len(given) + 2) + specs,
            [VM] * len(out_shape),
            scratch=[pltpu.VMEM((len(given), HALF, CHIP_COLS), BF16)],
            flops=2 * len(given) * HALF * CHIP_COLS * CHIP,
            size=len(given) * CHIP_COLS * CHIP * 2,
        )(*state, *[v for _, _, v in given], *weights, *extra)
    return state


def join_kernel(own_a, other_a, own_b, other_b, out_a, out_b):
    core = place()[2]
    for own, other, out in ((own_a, other_a, out_a), (own_b, other_b, out_b)):
        out[pl.ds(pl.multiple_of(core * HALF, HALF), HALF), :] = own[...]
        out[pl.ds(pl.multiple_of((1 - core) * HALF, HALF), HALF), :] = other[...]


def body(
    latents,
    input_weights,
    output_weights,
    position_table,
    level_scale,
    step_sizes,
    levels,
    group_order,
    group_mask,
):
    given = (levels, group_order, latents, level_scale, position_table)
    keep, send, keep_latents, send_latents = pl.pallas_call(
        first_kernel,
        out_shape=[sds((ROWS, FEAT), BF16)] * 2 + [sds((HALF, FEAT), F32)] * 2,
        in_specs=[HBM] * 5,
        out_specs=[VM] * 4,
        scratch_shapes=[pltpu.SMEM(v.shape, v.dtype) for v in given[:2]]
        + [pltpu.VMEM(v.shape, v.dtype) for v in given[2:]]
        + [pltpu.SemaphoreType.DMA((5,))],
        compiler_params=pltpu.CompilerParams(vmem_limit_bytes=62 * MB),
    )(*given)
    shard = call(pair_kernel, sds((2, ROWS, FEAT), BF16), [VM, VM, HBM], VM, limit=50)(
        keep, swap(send), input_weights
    )
    in_weights = [input_weights, swap(after(input_weights, shard))]

    for step in range(STEPS):
        sent = project(shard, in_weights, group_mask)
        if step == 0:
            out_weights = [output_weights, swap(after(output_weights, sent[0]))]
        pieces = [sent[0]] + [move_g(sent[4 - j], Z_MOVES[4 - j]) for j in (2, 1, 3)]
        pieces = [pieces[0], pieces[2], pieces[1], pieces[3]]
        other = swap(jnp.stack([v[0:HALF] for v in pieces]))
        near = jnp.stack([v[HALF : 3 * HALF].reshape(2, HALF, HD) for v in pieces], axis=1)
        below, above = move_g(near, Y_UP), move_g(near, Y_DOWN)
        far = move_g(below[0], Y_UP), move_g(above[1], Y_DOWN)
        state = attend(pieces, other, [(0, near[0], near[1])], [], False)
        blocks = [(3, below[0], below[1]), (1, above[0], above[1])]
        state = attend(pieces, other, blocks, state, False)
        mine, theirs = attend(pieces, other, [(2, *far)], state, True)
        attended = call(merge_kernel, [sds((HALF, HD), BF16)] * 4, [VM] * 2, [VM] * 4)(
            mine, swap(theirs)
        )
        if step == 0:
            scales = [level_scale, swap(after(level_scale, attended[0]))]
            tables = [position_table, swap(after(position_table, attended[0]))]
            dens = [keep_latents, swap(after(send_latents, attended[0]))]
        attended = [attended[0]] + [move_g(attended[4 - j], Z_MOVES[4 - j]) for j in (1, 2, 3)]
        result = output(
            jnp.stack(attended),
            out_weights,
            step,
            levels,
            group_order,
            step_sizes,
            dens,
            scales,
            tables,
        )
        dens = result[:2]
        shard = result[2]
    return tuple(
        call(
            join_kernel,
            [sds((2 * HALF, FEAT), F32), sds((2 * HALF, FEAT), BF16)],
            [VM] * 4,
            [VM] * 2,
        )(result[0], swap(result[1]), result[2], swap(result[3]))
    )


def solution(mesh):
    placed = (
        P("group", "tensor"),
        P(None, None, "tensor"),
        P(None, "tensor"),
        P(None, "tensor"),
        P(None, "tensor"),
        P(),
        P("group", None),
        P("group"),
        P("group", None),
    )
    return jax.shard_map(
        body,
        mesh=mesh,
        in_specs=placed,
        out_specs=(P("group", "tensor"), P("group", "tensor")),
        check_vma=False,
    )
```

```python
import functools
import math

import jax
import jax.numpy as jnp
from jax import lax
from jax.experimental import pallas as pl
from jax.experimental.pallas import tpu as pltpu
from jax.sharding import PartitionSpec as P


D = 6144
HD = 128
STEPS = 2
HALF = 128
FEAT = 384
CHIP = 2 * FEAT
COLS = 256
CHIP_COLS = 2 * COLS
ROWS = HALF + 16
PIECE = 3 * HALF
SHARD = 2 * HALF + 16
NEG = -1e30
F32 = jnp.float32
BF16 = jnp.bfloat16
VM = pl.BlockSpec(memory_space=pltpu.VMEM)
HBM = pl.BlockSpec(memory_space=pltpu.HBM)
SM = pl.BlockSpec(memory_space=pltpu.SMEM)
MB = 1 << 20
QUERIES = 4 * HALF
CHUNK = 256
BOTH = ("group", "tensor")


def t_perm(move):
    pairs = []
    for t in range(16):
        x, l, c = move(t // 4, t // 2 % 2, t % 2)
        pairs.append((t, (x % 4) * 4 + l * 2 + c))
    return pairs


def g_perm(dy, dz):
    return [(g, (g // 4 + dy) % 4 * 4 + (g + dz) % 4) for g in range(16)]


X_UP = t_perm(lambda x, l, c: (x + 1, l, c))
X_DOWN = t_perm(lambda x, l, c: (x - 1, l, c))
X_FAR = t_perm(lambda x, l, c: (x + 2, l, c))
Z_SWAP = t_perm(lambda x, l, c: (x, 1 - l, c))
C_SWAP = t_perm(lambda x, l, c: (x, l, 1 - c))
Y_UP, Y_DOWN, Y_FAR = g_perm(1, 0), g_perm(-1, 0), g_perm(2, 0)
Z_MOVES = {1: g_perm(0, 1), 2: g_perm(0, 2), 3: g_perm(0, -1)}


def move_t(array, pairs):
    return lax.ppermute(array, "tensor", pairs)


def move_g(array, pairs):
    return lax.ppermute(array, "group", pairs)


def swap(array):
    return lax.ppermute(array, "tensor", C_SWAP)


def after(array, *others):
    return lax.optimization_barrier((array, *others))[0]


def sds(shape, dtype):
    return jax.ShapeDtypeStruct(shape, dtype)


def call(kernel, out_shape, in_specs, out_specs, scratch=(), limit=12, flops=0, size=0):
    return pl.pallas_call(
        kernel,
        out_shape=out_shape,
        in_specs=in_specs,
        out_specs=out_specs,
        scratch_shapes=scratch,
        compiler_params=pltpu.CompilerParams(vmem_limit_bytes=limit * MB),
        cost_estimate=pl.CostEstimate(flops=flops, bytes_accessed=size, transcendentals=0),
    )


def place():
    t, g = lax.axis_index("tensor"), lax.axis_index("group")
    return t // 4, t // 2 % 2, t % 2, g // 4, g % 4


def modulated(shifted_from, level, order, scale_ref, table_ref):
    table = table_ref[...].astype(F32)
    row_at = lax.broadcasted_iota(jnp.int32, table.shape, 0)
    position = jnp.sum(jnp.where(row_at == order, table, 0.0), axis=0, keepdims=True)
    shifted = shifted_from + position
    factor = 1.0 + scale_ref[pl.ds(level, 1), :]
    squares = jnp.sum(shifted * shifted, axis=1, keepdims=True)
    lanes = jnp.transpose(jnp.broadcast_to(squares, (HALF, HALF)))[0:16, :]
    return (shifted * factor).astype(BF16), lanes


def store_squares(out, lanes):
    rows = out.shape[0]
    high = lanes.astype(BF16).astype(F32)
    middle = (lanes - high).astype(BF16).astype(F32)
    low = lanes - high - middle
    at = lax.broadcasted_iota(jnp.int32, lanes.shape, 0)
    parts = jnp.where(at == 0, high, jnp.where(at == 1, middle, jnp.where(at == 2, low, 0.0)))
    out[rows - 16 : rows, 0:HALF] = parts.astype(BF16)
    out[rows - 16 : rows, HALF:FEAT] = jnp.zeros((16, FEAT - HALF), BF16)


def load_squares(ref):
    rows = ref.shape[0]
    return jnp.sum(ref[rows - 16 : rows, 0:HALF].astype(F32), axis=0, keepdims=True)


def first_kernel(*refs):
    sources, outs, held, sems = refs[:5], refs[5:9], refs[9:14], refs[14]
    copies = [
        pltpu.make_async_copy(source, target, sems.at[i])
        for i, (source, target) in enumerate(zip(sources, held))
    ]
    for copy in copies:
        copy.start()
    for copy in copies:
        copy.wait()
    levels, order, latents, scale, table = held
    keep, send, keep_latents, send_latents = outs
    core = place()[2]
    for half, out, out_latents in ((core, keep, keep_latents), (1 - core, send, send_latents)):
        rows = latents[pl.ds(pl.multiple_of(half * HALF, HALF), HALF), :]
        out_latents[...] = rows
        out[0:HALF, :], lanes = modulated(rows, levels[0, 0], order[0], scale, table)
        store_squares(out, lanes)


def pair_kernel(own_hbm, other, weights, out, own, sem):
    copy = pltpu.make_async_copy(own_hbm, own, sem)
    copy.start()
    copy.wait()
    core = place()[2]
    for f, ref in ((core, own), (1 - core, other)):
        out[pl.ds(pl.multiple_of(f * HALF, HALF), HALF), :] = ref[0:HALF, :]
    store_squares(out, jnp.broadcast_to(load_squares(own) + load_squares(other), (16, HALF)))


def gather_rounds(shard):
    z = move_t(shard, Z_SWAP)
    far = move_t(shard, X_FAR)
    left, right = move_t(shard, X_UP), move_t(shard, X_DOWN)
    z_left, z_right = move_t(z, X_UP), move_t(z, X_DOWN)
    z_far = move_t(far, Z_SWAP)
    return [
        [(0, False, shard), (0, True, z), (3, False, left), (1, False, right)],
        [(2, False, far), (3, True, z_left), (1, True, z_right)],
        [(2, True, z_far)],
    ]


def chip_of(x, l, dx, other):
    return lax.rem(x + dx, 4) * 2 + (1 - l if other else l)


def project_kernel(*refs, shards, first, last, masked):
    refs = list(refs)
    total_in = square_in = None
    if not first:
        total_in, square_in = refs[:2]
        refs = refs[2:]
    given = refs[: len(shards)]
    weights = refs[len(shards) : len(shards) + 2]
    outs = refs[len(shards) + 2 :]
    if masked:
        mask_ref, outs = outs[0], outs[1:]
    x, l, core, _, z = place()
    lhs, starts = [], []
    square = jnp.zeros((8, HALF), F32) if first else square_in[...]
    for (dx, other), shard in zip(shards, given):
        lhs.append(jnp.concatenate([shard[0:HALF, :], shard[HALF : 2 * HALF, :]], axis=1))
        starts.append(pl.multiple_of(chip_of(x, l, dx, other) * CHIP, CHIP))
        square = square + jnp.broadcast_to(load_squares(shard), square.shape)
    if last:
        total = outs[4]
        rstd = lax.rsqrt(square[0:1, :] / D + 1e-06)
        rstd = jnp.transpose(jnp.broadcast_to(rstd, (HALF, HALF)))
        rstd = jnp.concatenate([rstd, rstd], axis=1)
    else:
        total = outs[0]
        outs[1][...] = square
    for s in range(2):
        for i in range(3):
            acc = None if first else total_in[s, i]
            for row, start in zip(lhs, starts):
                part = jnp.dot(row, weights[s][i, pl.ds(start, CHIP), :], preferred_element_type=F32)
                acc = part if acc is None else acc + part
            if last:
                acc = acc * rstd
                if i == 0:
                    acc = acc * (math.log2(math.e) / math.sqrt(HD))
            total[s, i] = acc
    if last:
        for j in range(4):
            head = lax.rem(z + j, 4)
            which = jnp.where(head // 2 == core, 0, 1)
            cols = pl.ds(pl.multiple_of(lax.rem(head, 2) * HD, HD), HD)
            for i in range(3):
                outs[j][i * HALF : (i + 1) * HALF, :] = total[which, i, :, cols].astype(BF16)
            if masked:
                mask = (mask_ref[...] > 0).astype(F32)
                outs[j][PIECE : PIECE + 16, :] = jnp.zeros((16, HD), BF16)
                outs[j][PIECE : PIECE + 16, 0:16] = jnp.broadcast_to(mask, (16, 16)).astype(BF16)


def project(shard, weights, mask):
    state = []
    rounds = gather_rounds(shard)
    for number, given in enumerate(rounds):
        first, last = number == 0, number == len(rounds) - 1
        shards = [(dx, other) for dx, other, _ in given]
        totals = [sds((2, 3, HALF, COLS), F32), sds((8, HALF), F32)]
        extra = mask if last else []
        out_shape = [sds((PIECE + 16 * len(extra), HD), BF16)] * 4 if last else totals
        state = call(
            functools.partial(
                project_kernel, shards=shards, first=first, last=last, masked=bool(extra)
            ),
            out_shape,
            [VM] * (len(state) + len(given) + 2 + len(extra)),
            [VM] * len(out_shape),
            scratch=[pltpu.VMEM(totals[0].shape, F32)] if last else [],
            flops=2 * len(given) * HALF * CHIP * 6 * COLS,
            size=len(given) * CHIP * 6 * COLS * 2,
        )(*state, *[v for _, _, v in given], *weights, *extra)
    return state


def attend_kernel(*refs, offsets, first, last):
    refs = list(refs)
    pieces, mask_refs, other = refs[:4], refs[4:8], refs[8]
    count = len(offsets)
    keys, values = refs[9 : 9 + count], refs[9 + count : 9 + 2 * count]
    refs = refs[9 + 2 * count :]
    if not first:
        top_in, sum_in, total_in = refs[:3]
        refs = refs[3:]
    _, _, _, y, z = place()
    masks = [ref[...].astype(F32)[0:1, :] for ref in mask_refs]
    lane = lax.broadcasted_iota(jnp.int32, (1, HD), 1)
    masks = [
        jnp.broadcast_to(jnp.where(lane < 16, (1.0 - m) * NEG, 0.0), (HALF, HD)).astype(BF16)
        for m in masks
    ]
    group_at = lax.broadcasted_iota(jnp.int32, (QUERIES, HD), 1)
    key_at = lax.broadcasted_iota(jnp.int32, (QUERIES, HD), 0)
    wide = []
    for dy, key in zip(offsets, keys):
        group = lax.rem(y + dy, 4) * 4 + lax.rem(z + key_at // HALF, 4)
        spread = jnp.where(group_at == group, 1.0, 0.0).astype(BF16)
        wide.append(jnp.concatenate([key[...].reshape(QUERIES, HD), spread], axis=1))
    for r in range(2 * QUERIES // CHUNK):
        mine = r * CHUNK < QUERIES
        rows = slice(r * CHUNK, (r + 1) * CHUNK)
        p = r * CHUNK % QUERIES // HALF
        query = [pieces[p + i][0:HALF, :] if mine else other[p + i] for i in range(2)]
        query = [jnp.concatenate([query[i], masks[p + i]], axis=1) for i in range(2)]
        query = jnp.concatenate(query, axis=0)
        scores = [
            lax.dot_general(query, key, (((1,), (1,)), ((), ())), preferred_element_type=F32)
            for key in wide
        ]
        best = functools.reduce(
            jnp.maximum, [s[:, i * HD : (i + 1) * HD] for s in scores for i in range(4)]
        )
        best = jnp.max(best, axis=1, keepdims=True)
        if not first:
            old = top_in[rows, :]
            best = jnp.maximum(best, old[:, 0:1])
            shrink = jnp.exp2(old - best)
            summed, acc = sum_in[rows, :] * shrink, total_in[rows, :] * shrink
        for k, score in enumerate(scores):
            weight = jnp.exp2(score - best)
            parts = sum(weight[:, i * HD : (i + 1) * HD] for i in range(4))
            part = jnp.dot(
                weight.astype(BF16),
                values[k][...].reshape(QUERIES, HD),
                preferred_element_type=F32,
            )
            if first and k == 0:
                summed, acc = parts, part
            else:
                summed, acc = summed + parts, acc + part
        if not last:
            refs[0][rows, :] = jnp.broadcast_to(best, (CHUNK, HD))
            refs[1][rows, :] = summed
            refs[2][rows, :] = acc
            continue
        summed = jnp.sum(summed, axis=1, keepdims=True)
        result = acc / summed
        level = best + jnp.log2(summed)
        rows = slice(r * CHUNK % QUERIES, r * CHUNK % QUERIES + CHUNK)
        out = refs[0] if mine else refs[1]
        out[rows, :] = result
        for i in range(2):
            line = jnp.broadcast_to(level[i * HALF : (i + 1) * HALF, :], (HALF, HD))
            out[QUERIES + p + i : QUERIES + p + i + 1, :] = jnp.transpose(line)[0:1, :]


def attend(pieces, masks, other, blocks, state, last):
    offsets = [dy for dy, _, _ in blocks]
    out_shape = [sds((QUERIES + 8, HD), F32)] * 2 if last else [sds((2 * QUERIES, HD), F32)] * 3
    return call(
        functools.partial(attend_kernel, offsets=offsets, first=not state, last=last),
        out_shape,
        [VM] * (9 + 2 * len(blocks) + len(state)),
        [VM] * len(out_shape),
        limit=16,
        flops=4 * 1024 * 512 * len(blocks) * HD,
        size=MB,
    )(*pieces, *masks, other, *[k for _, k, _ in blocks], *[v for _, _, v in blocks], *state)


def merge_kernel(own, other, *outs):
    for p in range(4):
        rows = slice(p * HALF, (p + 1) * HALF)
        line = slice(QUERIES + p, QUERIES + p + 1)
        gap = jnp.transpose(jnp.broadcast_to(other[line, :] - own[line, :], (HALF, HD)))
        share = 1.0 / (1.0 + jnp.exp2(gap))
        outs[p][...] = (own[rows, :] * share + other[rows, :] * (1.0 - share)).astype(BF16)


def output_kernel(*refs, shards, first, last, step):
    refs = list(refs)
    if not first:
        total_in = refs[0]
        refs = refs[1:]
    given = refs[: len(shards)]
    weights = refs[len(shards) : len(shards) + 2]
    refs = refs[len(shards) + 2 :]
    if last:
        levels, order, sizes = refs[:3]
        dens, scales, tables = refs[3:5], refs[5:7], refs[7:9]
        outs = refs[9:-1]
    else:
        outs = refs[:-1]
    heads = refs[-1]
    x, l, core, _, z = place()
    starts = []
    for n, ((dx, other), shard) in enumerate(zip(shards, given)):
        starts.append(pl.multiple_of(chip_of(x, l, dx, other) * CHIP_COLS, CHIP_COLS))
        for j in range(4):
            cols = pl.ds(pl.multiple_of(lax.rem(z + j, 4) * HD, HD), HD)
            heads[n, :, cols] = shard[j]
    for s in range(2):
        acc = None if first else total_in[s]
        for n, start in enumerate(starts):
            part = jnp.dot(
                heads[n], weights[s][pl.ds(start, CHIP_COLS), :], preferred_element_type=F32
            )
            acc = part if acc is None else acc + part
        if not last:
            outs[0][s] = acc
            continue
        denoised = dens[s][...] + sizes[levels[0, step]] * acc
        outs[s][...] = denoised
        if step == STEPS - 1:
            outs[2 + s][...] = acc.astype(BF16)
        else:
            features, more = modulated(denoised, levels[0, step + 1], order[0], scales[s], tables[s])
            f = core if s == 0 else 1 - core
            outs[2][pl.ds(pl.multiple_of(f * HALF, HALF), HALF), :] = features
            lanes = more if s == 0 else lanes + more
    if last and step < STEPS - 1:
        store_squares(outs[2], lanes)


def output(attended, weights, step, levels, order, sizes, dens, scales, tables):
    state = []
    rounds = gather_rounds(attended)
    for number, given in enumerate(rounds):
        first, last = number == 0, number == len(rounds) - 1
        shards = [(dx, other) for dx, other, _ in given]
        out_shape, extra, specs = [sds((2, HALF, FEAT), F32)], [], []
        if last:
            out_shape = [sds((HALF, FEAT), F32)] * 2
            if step == STEPS - 1:
                out_shape = out_shape + [sds((HALF, FEAT), BF16)] * 2
            else:
                out_shape = out_shape + [sds((SHARD, FEAT), BF16)]
            extra = [levels, order, sizes, *dens, *scales, *tables]
            specs = [SM] * 3 + [VM] * 6
        state = call(
            functools.partial(output_kernel, shards=shards, first=first, last=last, step=step),
            out_shape,
            [VM] * (len(state) + len(given) + 2) + specs,
            [VM] * len(out_shape),
            scratch=[pltpu.VMEM((len(given), HALF, CHIP_COLS), BF16)],
            flops=2 * len(given) * HALF * CHIP_COLS * CHIP,
            size=len(given) * CHIP_COLS * CHIP * 2,
        )(*state, *[v for _, _, v in given], *weights, *extra)
    return state


def join_kernel(own_a, other_a, own_b, other_b, out_a, out_b):
    core = place()[2]
    for own, other, out in ((own_a, other_a, out_a), (own_b, other_b, out_b)):
        out[pl.ds(pl.multiple_of(core * HALF, HALF), HALF), :] = own[...]
        out[pl.ds(pl.multiple_of((1 - core) * HALF, HALF), HALF), :] = other[...]


def body(
    latents,
    input_weights,
    output_weights,
    position_table,
    level_scale,
    step_sizes,
    levels,
    group_order,
    group_mask,
):
    given = (levels, group_order, latents, level_scale, position_table)
    keep, send, keep_latents, send_latents = pl.pallas_call(
        first_kernel,
        out_shape=[sds((ROWS, FEAT), BF16)] * 2 + [sds((HALF, FEAT), F32)] * 2,
        in_specs=[HBM] * 5,
        out_specs=[VM] * 4,
        scratch_shapes=[pltpu.SMEM(v.shape, v.dtype) for v in given[:2]]
        + [pltpu.VMEM(v.shape, v.dtype) for v in given[2:]]
        + [pltpu.SemaphoreType.DMA((5,))],
        compiler_params=pltpu.CompilerParams(vmem_limit_bytes=62 * MB),
    )(*given)
    shard = call(
        pair_kernel,
        sds((SHARD, FEAT), BF16),
        [HBM, VM, HBM],
        VM,
        scratch=[pltpu.VMEM((ROWS, FEAT), BF16), pltpu.SemaphoreType.DMA],
        limit=50,
    )(keep, swap(send), input_weights)
    in_weights = [input_weights, swap(after(input_weights, shard))]

    for step in range(STEPS):
        sent = project(shard, in_weights, [] if step else [group_mask])
        pieces = [sent[0]] + [move_g(sent[4 - j], Z_MOVES[4 - j]) for j in (1, 2, 3)]
        if step == 0:
            masks = [v[PIECE:] for v in pieces]
        other = swap(jnp.stack([v[0:HALF] for v in pieces]))
        near = jnp.stack([v[HALF:PIECE].reshape(2, HALF, HD) for v in pieces], axis=1)
        below, above = move_g(near, Y_UP), move_g(near, Y_DOWN)
        state = attend(pieces, masks, other, [(0, near[0], near[1])], [], False)
        far = [
            move_g(after(below[0], *state), Y_UP),
            move_g(after(above[1], *state), Y_DOWN),
        ]
        blocks = [(3, below[0], below[1]), (1, above[0], above[1])]
        state = attend(pieces, masks, other, blocks, state, False)
        mine, theirs = attend(pieces, masks, other, [(2, *far)], state, True)
        attended = call(merge_kernel, [sds((HALF, HD), BF16)] * 4, [VM] * 2, [VM] * 4)(
            mine, swap(theirs)
        )
        if step == 0:
            out_weights = [output_weights, swap(after(output_weights, attended[0]))]
            scales = [level_scale, swap(after(level_scale, attended[0]))]
            tables = [position_table, swap(after(position_table, attended[0]))]
            dens = [keep_latents, swap(after(send_latents, attended[0]))]
        attended = [attended[0]] + [move_g(attended[4 - j], Z_MOVES[4 - j]) for j in (1, 2, 3)]
        result = output(
            jnp.stack(attended),
            out_weights,
            step,
            levels,
            group_order,
            step_sizes,
            dens,
            scales,
            tables,
        )
        dens = result[:2]
        shard = result[2]
    return tuple(
        call(
            join_kernel,
            [sds((2 * HALF, FEAT), F32), sds((2 * HALF, FEAT), BF16)],
            [VM] * 4,
            [VM] * 2,
        )(result[0], swap(result[1]), result[2], swap(result[3]))
    )


def solution(mesh):
    placed = (
        P("group", "tensor"),
        P(None, None, "tensor"),
        P(None, "tensor"),
        P(None, "tensor"),
        P(None, "tensor"),
        P(),
        P("group", None),
        P("group"),
        P("group", None),
    )
    return jax.shard_map(
        body,
        mesh=mesh,
        in_specs=placed,
        out_specs=(P("group", "tensor"), P("group", "tensor")),
        check_vma=False,
    )
```

```python
import functools
import math

import jax
import jax.numpy as jnp
from jax import lax
from jax.experimental import pallas as pl
from jax.experimental.pallas import tpu as pltpu
from jax.sharding import PartitionSpec as P


D = 6144
HD = 128
STEPS = 2
LEVELS = 32
HALF = 128
FEAT = 384
CHIP = 2 * FEAT
COLS = 256
CHIP_COLS = 2 * COLS
ROWS = HALF + 16
PIECE = 3 * HALF
SHARD = 2 * HALF + 16
NEG = -1e30
F32 = jnp.float32
BF16 = jnp.bfloat16
VM = pl.BlockSpec(memory_space=pltpu.VMEM)
HBM = pl.BlockSpec(memory_space=pltpu.HBM)
SM = pl.BlockSpec(memory_space=pltpu.SMEM)
MB = 1 << 20
QUERIES = 4 * HALF
CHUNK = 256


def t_perm(move):
    pairs = []
    for t in range(16):
        x, l, c = move(t // 4, t // 2 % 2, t % 2)
        pairs.append((t, (x % 4) * 4 + l * 2 + c))
    return pairs


def g_perm(dy, dz):
    return [(g, (g // 4 + dy) % 4 * 4 + (g + dz) % 4) for g in range(16)]


X_UP = t_perm(lambda x, l, c: (x + 1, l, c))
X_DOWN = t_perm(lambda x, l, c: (x - 1, l, c))
X_FAR = t_perm(lambda x, l, c: (x + 2, l, c))
Z_SWAP = t_perm(lambda x, l, c: (x, 1 - l, c))
C_SWAP = t_perm(lambda x, l, c: (x, l, 1 - c))
Y_UP, Y_DOWN, Y_FAR = g_perm(1, 0), g_perm(-1, 0), g_perm(2, 0)
Z_MOVES = {1: g_perm(0, 1), 2: g_perm(0, 2), 3: g_perm(0, -1)}


def move_t(array, pairs):
    return lax.ppermute(array, "tensor", pairs)


def move_g(array, pairs):
    return lax.ppermute(array, "group", pairs)


def swap(array):
    return lax.ppermute(array, "tensor", C_SWAP)


def turned(index):
    return lax.rem(index, 2) * 2 + index // 2


def stack(pieces, axis):
    early = jnp.stack([pieces[0], pieces[2]], axis=axis)
    late = jnp.stack([pieces[1], pieces[3]], axis=axis)
    return jnp.concatenate([after(early), late], axis=axis)


def after(array, *others):
    return lax.optimization_barrier((array, *others))[0]


def sds(shape, dtype):
    return jax.ShapeDtypeStruct(shape, dtype)


def call(kernel, out_shape, in_specs, out_specs, scratch=(), limit=12, flops=0, size=0):
    return pl.pallas_call(
        kernel,
        out_shape=out_shape,
        in_specs=in_specs,
        out_specs=out_specs,
        scratch_shapes=scratch,
        compiler_params=pltpu.CompilerParams(vmem_limit_bytes=limit * MB),
        cost_estimate=pl.CostEstimate(flops=flops, bytes_accessed=size, transcendentals=0),
    )


def place():
    t, g = lax.axis_index("tensor"), lax.axis_index("group")
    return t // 4, t // 2 % 2, t % 2, g // 4, g % 4


def modulated(shifted_from, level, order, scale_ref, table_ref):
    table = table_ref[...].astype(F32)
    row_at = lax.broadcasted_iota(jnp.int32, table.shape, 0)
    position = jnp.sum(jnp.where(row_at == order, table, 0.0), axis=0, keepdims=True)
    shifted = shifted_from + position
    factor = 1.0 + scale_ref[pl.ds(level, 1), :]
    squares = jnp.sum(shifted * shifted, axis=1, keepdims=True)
    lanes = jnp.transpose(jnp.broadcast_to(squares, (HALF, HALF)))[0:16, :]
    return (shifted * factor).astype(BF16), lanes


def store_squares(out, lanes):
    rows = out.shape[0]
    high = lanes.astype(BF16).astype(F32)
    middle = (lanes - high).astype(BF16).astype(F32)
    low = lanes - high - middle
    at = lax.broadcasted_iota(jnp.int32, lanes.shape, 0)
    parts = jnp.where(at == 0, high, jnp.where(at == 1, middle, jnp.where(at == 2, low, 0.0)))
    out[rows - 16 : rows, 0:HALF] = parts.astype(BF16)
    out[rows - 16 : rows, HALF:FEAT] = jnp.zeros((16, FEAT - HALF), BF16)


def load_squares(ref):
    rows = ref.shape[0]
    return jnp.sum(ref[rows - 16 : rows, 0:HALF].astype(F32), axis=0, keepdims=True)


def first_kernel(*refs):
    sources, outs, held, sems = refs[:5], refs[5:9], refs[9:14], refs[14]
    copies = [
        pltpu.make_async_copy(source, target, sems.at[i])
        for i, (source, target) in enumerate(zip(sources, held))
    ]
    for copy in copies:
        copy.start()
    for copy in copies:
        copy.wait()
    levels, order, latents, scale, table = held
    keep, send, keep_latents, send_latents = outs
    core = place()[2]
    for half, out, out_latents in ((core, keep, keep_latents), (1 - core, send, send_latents)):
        rows = latents[pl.ds(pl.multiple_of(half * HALF, HALF), HALF), :]
        out_latents[...] = rows
        out[0:HALF, :], lanes = modulated(rows, levels[0, 0], order[0], scale, table)
        store_squares(out, lanes)


def pair_kernel(own_hbm, other, weights, out, own, sem):
    copy = pltpu.make_async_copy(own_hbm, own, sem)
    copy.start()
    copy.wait()
    core = place()[2]
    for f, ref in ((core, own), (1 - core, other)):
        out[pl.ds(pl.multiple_of(f * HALF, HALF), HALF), :] = ref[0:HALF, :]
    store_squares(out, jnp.broadcast_to(load_squares(own) + load_squares(other), (16, HALF)))


def gather_rounds(shard):
    z = move_t(shard, Z_SWAP)
    far = move_t(shard, X_FAR)
    left, right = move_t(shard, X_UP), move_t(shard, X_DOWN)
    z_left, z_right = move_t(z, X_UP), move_t(z, X_DOWN)
    z_far = move_t(far, Z_SWAP)
    return [
        [(0, False, shard), (0, True, z), (3, False, left), (1, False, right)],
        [(2, False, far), (2, True, z_far)],
        [(3, True, z_left), (1, True, z_right)],
    ]


def chip_of(x, l, dx, other):
    return lax.rem(x + dx, 4) * 2 + (1 - l if other else l)


def project_kernel(*refs, shards, first, last, masked):
    refs = list(refs)
    total_in = square_in = None
    if not first:
        total_in, square_in = refs[:2]
        refs = refs[2:]
    given = refs[: len(shards)]
    weights = refs[len(shards) : len(shards) + 2]
    outs = refs[len(shards) + 2 :]
    if masked:
        mask_ref, outs = outs[0], outs[1:]
    x, l, core, _, z = place()
    lhs, starts = [], []
    square = jnp.zeros((8, HALF), F32) if first else square_in[...]
    for (dx, other), shard in zip(shards, given):
        lhs.append(jnp.concatenate([shard[0:HALF, :], shard[HALF : 2 * HALF, :]], axis=1))
        starts.append(pl.multiple_of(chip_of(x, l, dx, other) * CHIP, CHIP))
        square = square + jnp.broadcast_to(load_squares(shard), square.shape)
    if last:
        total = outs[4]
        rstd = lax.rsqrt(square[0:1, :] / D + 1e-06)
        rstd = jnp.transpose(jnp.broadcast_to(rstd, (HALF, HALF)))
        rstd = jnp.concatenate([rstd, rstd], axis=1)
    else:
        total = outs[0]
        outs[1][...] = square
    for s in range(2):
        for i in range(3):
            acc = None if first else total_in[s, i]
            for row, start in zip(lhs, starts):
                part = jnp.dot(row, weights[s][i, pl.ds(start, CHIP), :], preferred_element_type=F32)
                acc = part if acc is None else acc + part
            if last:
                acc = acc * rstd
                if i == 0:
                    acc = acc * (math.log2(math.e) / math.sqrt(HD))
            total[s, i] = acc
    if last:
        for j in range(4):
            head = lax.rem(z + j, 4)
            which = jnp.where(head // 2 == core, 0, 1)
            cols = pl.ds(pl.multiple_of(lax.rem(head, 2) * HD, HD), HD)
            for i in range(3):
                outs[j][i * HALF : (i + 1) * HALF, :] = total[which, i, :, cols].astype(BF16)
            if masked:
                mask = (mask_ref[...] > 0).astype(F32)
                outs[j][PIECE : PIECE + 16, :] = jnp.zeros((16, HD), BF16)
                outs[j][PIECE : PIECE + 16, 0:16] = jnp.broadcast_to(mask, (16, 16)).astype(BF16)


def project(shard, weights, mask):
    state = []
    rounds = gather_rounds(shard)
    for number, given in enumerate(rounds):
        first, last = number == 0, number == len(rounds) - 1
        shards = [(dx, other) for dx, other, _ in given]
        totals = [sds((2, 3, HALF, COLS), F32), sds((8, HALF), F32)]
        extra = mask if last else []
        out_shape = [sds((PIECE + 16 * len(extra), HD), BF16)] * 4 if last else totals
        state = call(
            functools.partial(
                project_kernel, shards=shards, first=first, last=last, masked=bool(extra)
            ),
            out_shape,
            [VM] * (len(state) + len(given) + 2 + len(extra)),
            [VM] * len(out_shape),
            scratch=[pltpu.VMEM(totals[0].shape, F32)] if last else [],
            flops=2 * len(given) * HALF * CHIP * 6 * COLS,
            size=len(given) * CHIP * 6 * COLS * 2,
        )(*state, *[v for _, _, v in given], *weights, *extra)
    return state


def attend_kernel(*refs, offsets, first, last):
    refs = list(refs)
    pieces, mask_refs, other = refs[:4], refs[4:8], refs[8]
    count = len(offsets)
    keys, values = refs[9 : 9 + count], refs[9 + count : 9 + 2 * count]
    refs = refs[9 + 2 * count :]
    if not first:
        top_in, sum_in, total_in = refs[:3]
        refs = refs[3:]
    _, _, _, y, z = place()
    masks = [ref[...].astype(F32)[0:1, :] for ref in mask_refs]
    lane = lax.broadcasted_iota(jnp.int32, (1, HD), 1)
    masks = [
        jnp.broadcast_to(jnp.where(lane < 16, (1.0 - m) * NEG, 0.0), (HALF, HD)).astype(BF16)
        for m in masks
    ]
    group_at = lax.broadcasted_iota(jnp.int32, (QUERIES, HD), 1)
    key_at = lax.broadcasted_iota(jnp.int32, (QUERIES, HD), 0)
    wide = []
    for dy, key in zip(offsets, keys):
        group = lax.rem(y + dy, 4) * 4 + lax.rem(z + turned(key_at // HALF), 4)
        spread = jnp.where(group_at == group, 1.0, 0.0).astype(BF16)
        wide.append(jnp.concatenate([key[...].reshape(QUERIES, HD), spread], axis=1))
    for r in range(2 * QUERIES // CHUNK):
        mine = r * CHUNK < QUERIES
        rows = slice(r * CHUNK, (r + 1) * CHUNK)
        p = r * CHUNK % QUERIES // HALF
        query = [pieces[p + i][0:HALF, :] if mine else other[p + i] for i in range(2)]
        query = [jnp.concatenate([query[i], masks[p + i]], axis=1) for i in range(2)]
        query = jnp.concatenate(query, axis=0)
        scores = [
            lax.dot_general(query, key, (((1,), (1,)), ((), ())), preferred_element_type=F32)
            for key in wide
        ]
        best = functools.reduce(
            jnp.maximum, [s[:, i * HD : (i + 1) * HD] for s in scores for i in range(4)]
        )
        best = jnp.max(best, axis=1, keepdims=True)
        if not first:
            old = top_in[rows, :]
            best = jnp.maximum(best, old[:, 0:1])
            shrink = jnp.exp2(old - best)
            summed, acc = sum_in[rows, :] * shrink, total_in[rows, :] * shrink
        for k, score in enumerate(scores):
            weight = jnp.exp2(score - best)
            parts = sum(weight[:, i * HD : (i + 1) * HD] for i in range(4))
            part = jnp.dot(
                weight.astype(BF16),
                values[k][...].reshape(QUERIES, HD),
                preferred_element_type=F32,
            )
            if first and k == 0:
                summed, acc = parts, part
            else:
                summed, acc = summed + parts, acc + part
        if not last:
            refs[0][rows, :] = jnp.broadcast_to(best, (CHUNK, HD))
            refs[1][rows, :] = summed
            refs[2][rows, :] = acc
            continue
        summed = jnp.sum(summed, axis=1, keepdims=True)
        result = acc / summed
        level = best + jnp.log2(summed)
        rows = slice(r * CHUNK % QUERIES, r * CHUNK % QUERIES + CHUNK)
        out = refs[0] if mine else refs[1]
        out[rows, :] = result
        for i in range(2):
            line = jnp.broadcast_to(level[i * HALF : (i + 1) * HALF, :], (HALF, HD))
            out[QUERIES + p + i : QUERIES + p + i + 1, :] = jnp.transpose(line)[0:1, :]


def attend(pieces, masks, other, blocks, state, last):
    offsets = [dy for dy, _, _ in blocks]
    out_shape = [sds((QUERIES + 8, HD), F32)] * 2 if last else [sds((2 * QUERIES, HD), F32)] * 3
    return call(
        functools.partial(attend_kernel, offsets=offsets, first=not state, last=last),
        out_shape,
        [VM] * (9 + 2 * len(blocks) + len(state)),
        [VM] * len(out_shape),
        limit=16,
        flops=4 * 1024 * 512 * len(blocks) * HD,
        size=MB,
    )(*pieces, *masks, other, *[k for _, k, _ in blocks], *[v for _, _, v in blocks], *state)


def merge_kernel(own, other, *outs):
    for p in range(4):
        rows = slice(p * HALF, (p + 1) * HALF)
        line = slice(QUERIES + p, QUERIES + p + 1)
        gap = jnp.transpose(jnp.broadcast_to(other[line, :] - own[line, :], (HALF, HD)))
        share = 1.0 / (1.0 + jnp.exp2(gap))
        outs[p][...] = (own[rows, :] * share + other[rows, :] * (1.0 - share)).astype(BF16)


def output_kernel(*refs, shards, first, last, step):
    refs = list(refs)
    if not first:
        total_in = refs[0]
        refs = refs[1:]
    given = refs[: len(shards)]
    weights = refs[len(shards) : len(shards) + 2]
    refs = refs[len(shards) + 2 :]
    if last:
        levels, order, sizes = refs[:3]
        dens, scales, tables = refs[3:5], refs[5:7], refs[7:9]
        outs = refs[9:-1]
    else:
        outs = refs[:-1]
    heads = refs[-1]
    x, l, core, _, z = place()
    starts = []
    for n, ((dx, other), shard) in enumerate(zip(shards, given)):
        starts.append(pl.multiple_of(chip_of(x, l, dx, other) * CHIP_COLS, CHIP_COLS))
        for j in range(4):
            cols = pl.ds(pl.multiple_of(lax.rem(z + (0, 2, 1, 3)[j], 4) * HD, HD), HD)
            heads[n, :, cols] = shard[j]
    for s in range(2):
        acc = None if first else total_in[s]
        for n, start in enumerate(starts):
            part = jnp.dot(
                heads[n], weights[s][pl.ds(start, CHIP_COLS), :], preferred_element_type=F32
            )
            acc = part if acc is None else acc + part
        if not last:
            outs[0][s] = acc
            continue
        denoised = dens[s][...] + sizes[levels[0, step]] * acc
        outs[s][...] = denoised
        if step == STEPS - 1:
            outs[2 + s][...] = acc.astype(BF16)
        else:
            features, more = modulated(denoised, levels[0, step + 1], order[0], scales[s], tables[s])
            f = core if s == 0 else 1 - core
            outs[2][pl.ds(pl.multiple_of(f * HALF, HALF), HALF), :] = features
            lanes = more if s == 0 else lanes + more
    if last and step < STEPS - 1:
        store_squares(outs[2], lanes)


def output(attended, weights, step, levels, order, sizes, dens, scales, tables):
    state = []
    rounds = gather_rounds(attended)
    for number, given in enumerate(rounds):
        first, last = number == 0, number == len(rounds) - 1
        shards = [(dx, other) for dx, other, _ in given]
        out_shape, extra, specs = [sds((2, HALF, FEAT), F32)], [], []
        if last:
            out_shape = [sds((HALF, FEAT), F32)] * 2
            if step == STEPS - 1:
                out_shape = out_shape + [sds((HALF, FEAT), BF16)] * 2
            else:
                out_shape = out_shape + [sds((SHARD, FEAT), BF16)]
            extra = [levels, order, sizes, *dens, *scales, *tables]
            specs = [SM] * 3 + [VM] * 6
        state = call(
            functools.partial(output_kernel, shards=shards, first=first, last=last, step=step),
            out_shape,
            [VM] * (len(state) + len(given) + 2) + specs,
            [VM] * len(out_shape),
            scratch=[pltpu.VMEM((len(given), HALF, CHIP_COLS), BF16)],
            flops=2 * len(given) * HALF * CHIP_COLS * CHIP,
            size=len(given) * CHIP_COLS * CHIP * 2,
        )(*state, *[v for _, _, v in given], *weights, *extra)
    return state


def join_kernel(own_a, other_a, own_b, other_b, out_a, out_b):
    core = place()[2]
    for own, other, out in ((own_a, other_a, out_a), (own_b, other_b, out_b)):
        out[pl.ds(pl.multiple_of(core * HALF, HALF), HALF), :] = own[...]
        out[pl.ds(pl.multiple_of((1 - core) * HALF, HALF), HALF), :] = other[...]


def body(
    latents,
    input_weights,
    output_weights,
    position_table,
    level_scale,
    step_sizes,
    levels,
    group_order,
    group_mask,
):
    given = (levels, group_order, latents, level_scale, position_table)
    keep, send, keep_latents, send_latents = pl.pallas_call(
        first_kernel,
        out_shape=[sds((ROWS, FEAT), BF16)] * 2 + [sds((HALF, FEAT), F32)] * 2,
        in_specs=[HBM] * 5,
        out_specs=[VM] * 4,
        scratch_shapes=[pltpu.SMEM(v.shape, v.dtype) for v in given[:2]]
        + [pltpu.VMEM(v.shape, v.dtype) for v in given[2:]]
        + [pltpu.SemaphoreType.DMA((5,))],
        compiler_params=pltpu.CompilerParams(vmem_limit_bytes=62 * MB),
    )(*given)
    shard = call(
        pair_kernel,
        sds((SHARD, FEAT), BF16),
        [HBM, VM, HBM],
        VM,
        scratch=[pltpu.VMEM((ROWS, FEAT), BF16), pltpu.SemaphoreType.DMA],
        limit=50,
    )(keep, swap(send), input_weights)
    packed = [send_latents, level_scale, position_table.astype(F32)]
    packed = jnp.concatenate(packed, axis=0)
    in_weights = [input_weights, swap(after(input_weights, shard))]

    for step in range(STEPS):
        sent = project(shard, in_weights, [] if step else [group_mask])
        pieces = [sent[0]] + [move_g(sent[4 - j], Z_MOVES[4 - j]) for j in (1, 2, 3)]
        if step == 0:
            packed = swap(after(packed, sent[0]))
            scales = [level_scale, packed[HALF : HALF + LEVELS]]
            tables = [position_table, packed[HALF + LEVELS :]]
            dens = [keep_latents, packed[:HALF]]
            masks = [v[PIECE:] for v in pieces]
        other = swap(jnp.stack([v[0:HALF] for v in pieces]))
        near = stack([v[HALF:PIECE].reshape(2, HALF, HD) for v in pieces], 1)
        below, above = move_g(near, Y_UP), move_g(near, Y_DOWN)
        state = attend(pieces, masks, other, [(0, near[0], near[1])], [], False)
        far = [
            move_g(after(below[0], *state), Y_UP),
            move_g(after(above[1], *state), Y_DOWN),
        ]
        blocks = [(3, below[0], below[1]), (1, above[0], above[1])]
        state = attend(pieces, masks, other, blocks, state, False)
        mine, theirs = attend(pieces, masks, other, [(2, *far)], state, True)
        attended = call(merge_kernel, [sds((HALF, HD), BF16)] * 4, [VM] * 2, [VM] * 4)(
            mine, swap(theirs)
        )
        if step == 0:
            out_weights = [output_weights, swap(after(output_weights, attended[0]))]
        attended = [attended[0]] + [move_g(attended[4 - j], Z_MOVES[4 - j]) for j in (1, 2, 3)]
        result = output(
            stack(attended, 0),
            out_weights,
            step,
            levels,
            group_order,
            step_sizes,
            dens,
            scales,
            tables,
        )
        dens = result[:2]
        shard = result[2]
    return tuple(
        call(
            join_kernel,
            [sds((2 * HALF, FEAT), F32), sds((2 * HALF, FEAT), BF16)],
            [VM] * 4,
            [VM] * 2,
        )(result[0], swap(result[1]), result[2], swap(result[3]))
    )


def solution(mesh):
    placed = (
        P("group", "tensor"),
        P(None, None, "tensor"),
        P(None, "tensor"),
        P(None, "tensor"),
        P(None, "tensor"),
        P(),
        P("group", None),
        P("group"),
        P("group", None),
    )
    return jax.shard_map(
        body,
        mesh=mesh,
        in_specs=placed,
        out_specs=(P("group", "tensor"), P("group", "tensor")),
        check_vma=False,
    )
```

```python
import functools
import math

import jax
import jax.numpy as jnp
from jax import lax
from jax.experimental import pallas as pl
from jax.experimental.pallas import tpu as pltpu
from jax.sharding import PartitionSpec as P


D = 6144
HD = 128
STEPS = 2
LEVELS = 32
HALF = 128
FEAT = 384
CHIP = 2 * FEAT
COLS = 256
CHIP_COLS = 2 * COLS
ROWS = HALF + 16
PIECE = 3 * HALF
SHARD = 2 * HALF + 16
NEG = -1e30
F32 = jnp.float32
BF16 = jnp.bfloat16
VM = pl.BlockSpec(memory_space=pltpu.VMEM)
HBM = pl.BlockSpec(memory_space=pltpu.HBM)
SM = pl.BlockSpec(memory_space=pltpu.SMEM)
MB = 1 << 20
QUERIES = 4 * HALF
CHUNK = 256


def t_perm(move):
    pairs = []
    for t in range(16):
        x, l, c = move(t // 4, t // 2 % 2, t % 2)
        pairs.append((t, (x % 4) * 4 + l * 2 + c))
    return pairs


def g_perm(dy, dz):
    return [(g, (g // 4 + dy) % 4 * 4 + (g + dz) % 4) for g in range(16)]


X_UP = t_perm(lambda x, l, c: (x + 1, l, c))
X_DOWN = t_perm(lambda x, l, c: (x - 1, l, c))
X_FAR = t_perm(lambda x, l, c: (x + 2, l, c))
Z_SWAP = t_perm(lambda x, l, c: (x, 1 - l, c))
C_SWAP = t_perm(lambda x, l, c: (x, l, 1 - c))
Y_UP, Y_DOWN = g_perm(1, 0), g_perm(-1, 0)
ONWARD = [
    (g * 16 + t, (Y_DOWN if t % 2 else Y_UP)[g][1] * 16 + t) for g in range(16) for t in range(16)
]
Z_MOVES = {1: g_perm(0, 1), 2: g_perm(0, 2), 3: g_perm(0, -1)}


def move_t(array, pairs):
    return lax.ppermute(array, "tensor", pairs)


def move_g(array, pairs):
    return lax.ppermute(array, "group", pairs)


def swap(array):
    return lax.ppermute(array, "tensor", C_SWAP)


def turned(index):
    return lax.rem(index, 2) * 2 + index // 2


def stack(pieces, axis):
    early = jnp.stack([pieces[0], pieces[2]], axis=axis)
    late = jnp.stack([pieces[1], pieces[3]], axis=axis)
    return jnp.concatenate([after(early), late], axis=axis)


def after(array, *others):
    return lax.optimization_barrier((array, *others))[0]


def sds(shape, dtype):
    return jax.ShapeDtypeStruct(shape, dtype)


def call(kernel, out_shape, in_specs, out_specs, scratch=(), limit=12, flops=0, size=0):
    return pl.pallas_call(
        kernel,
        out_shape=out_shape,
        in_specs=in_specs,
        out_specs=out_specs,
        scratch_shapes=scratch,
        compiler_params=pltpu.CompilerParams(vmem_limit_bytes=limit * MB),
        cost_estimate=pl.CostEstimate(flops=flops, bytes_accessed=size, transcendentals=0),
    )


def place():
    t, g = lax.axis_index("tensor"), lax.axis_index("group")
    return t // 4, t // 2 % 2, t % 2, g // 4, g % 4


def modulated(shifted_from, level, order, scale_ref, table_ref):
    table = table_ref[...].astype(F32)
    row_at = lax.broadcasted_iota(jnp.int32, table.shape, 0)
    position = jnp.sum(jnp.where(row_at == order, table, 0.0), axis=0, keepdims=True)
    shifted = shifted_from + position
    factor = 1.0 + scale_ref[pl.ds(level, 1), :]
    squares = jnp.sum(shifted * shifted, axis=1, keepdims=True)
    lanes = jnp.transpose(jnp.broadcast_to(squares, (HALF, HALF)))[0:16, :]
    return (shifted * factor).astype(BF16), lanes


def store_squares(out, lanes):
    rows = out.shape[0]
    high = lanes.astype(BF16).astype(F32)
    middle = (lanes - high).astype(BF16).astype(F32)
    low = lanes - high - middle
    at = lax.broadcasted_iota(jnp.int32, lanes.shape, 0)
    parts = jnp.where(at == 0, high, jnp.where(at == 1, middle, jnp.where(at == 2, low, 0.0)))
    out[rows - 16 : rows, 0:HALF] = parts.astype(BF16)
    out[rows - 16 : rows, HALF:FEAT] = jnp.zeros((16, FEAT - HALF), BF16)


def load_squares(ref):
    rows = ref.shape[0]
    return jnp.sum(ref[rows - 16 : rows, 0:HALF].astype(F32), axis=0, keepdims=True)


def first_kernel(*refs):
    sources, outs, held, sems = refs[:5], refs[5:9], refs[9:14], refs[14]
    copies = [
        pltpu.make_async_copy(source, target, sems.at[i])
        for i, (source, target) in enumerate(zip(sources, held))
    ]
    for copy in copies:
        copy.start()
    for copy in copies:
        copy.wait()
    levels, order, latents, scale, table = held
    keep, send, keep_latents, send_latents = outs
    core = place()[2]
    for half, out, out_latents in ((core, keep, keep_latents), (1 - core, send, send_latents)):
        rows = latents[pl.ds(pl.multiple_of(half * HALF, HALF), HALF), :]
        out_latents[...] = rows
        out[0:HALF, :], lanes = modulated(rows, levels[0, 0], order[0], scale, table)
        store_squares(out, lanes)


def pair_kernel(own_hbm, other, weights, out, own, sem):
    copy = pltpu.make_async_copy(own_hbm, own, sem)
    copy.start()
    copy.wait()
    core = place()[2]
    for f, ref in ((core, own), (1 - core, other)):
        out[pl.ds(pl.multiple_of(f * HALF, HALF), HALF), :] = ref[0:HALF, :]
    store_squares(out, jnp.broadcast_to(load_squares(own) + load_squares(other), (16, HALF)))


def gather_rounds(shard):
    z = move_t(shard, Z_SWAP)
    far = move_t(shard, X_FAR)
    left, right = move_t(shard, X_UP), move_t(shard, X_DOWN)
    z_left, z_right = move_t(z, X_UP), move_t(z, X_DOWN)
    z_far = move_t(far, Z_SWAP)
    return [
        [(0, False, shard), (0, True, z), (3, False, left), (1, False, right)],
        [(2, False, far), (2, True, z_far)],
        [(3, True, z_left), (1, True, z_right)],
    ]


def chip_of(x, l, dx, other):
    return lax.rem(x + dx, 4) * 2 + (1 - l if other else l)


def project_kernel(*refs, shards, first, last, masked):
    refs = list(refs)
    total_in = square_in = None
    if not first:
        total_in, square_in = refs[:2]
        refs = refs[2:]
    given = refs[: len(shards)]
    weights = refs[len(shards) : len(shards) + 2]
    outs = refs[len(shards) + 2 :]
    if masked:
        mask_ref, outs = outs[0], outs[1:]
    x, l, core, _, z = place()
    lhs, starts = [], []
    square = jnp.zeros((8, HALF), F32) if first else square_in[...]
    for (dx, other), shard in zip(shards, given):
        lhs.append(jnp.concatenate([shard[0:HALF, :], shard[HALF : 2 * HALF, :]], axis=1))
        starts.append(pl.multiple_of(chip_of(x, l, dx, other) * CHIP, CHIP))
        square = square + jnp.broadcast_to(load_squares(shard), square.shape)
    if last:
        total = outs[4]
        rstd = lax.rsqrt(square[0:1, :] / D + 1e-06)
        rstd = jnp.transpose(jnp.broadcast_to(rstd, (HALF, HALF)))
        rstd = jnp.concatenate([rstd, rstd], axis=1)
    else:
        total = outs[0]
        outs[1][...] = square
    for s in range(2):
        for i in range(3):
            acc = None if first else total_in[s, i]
            for row, start in zip(lhs, starts):
                part = jnp.dot(row, weights[s][i, pl.ds(start, CHIP), :], preferred_element_type=F32)
                acc = part if acc is None else acc + part
            if last:
                acc = acc * rstd
                if i == 0:
                    acc = acc * (math.log2(math.e) / math.sqrt(HD))
            total[s, i] = acc
    if last:
        for j in range(4):
            head = lax.rem(z + j, 4)
            which = jnp.where(head // 2 == core, 0, 1)
            cols = pl.ds(pl.multiple_of(lax.rem(head, 2) * HD, HD), HD)
            for i in range(3):
                outs[j][i * HALF : (i + 1) * HALF, :] = total[which, i, :, cols].astype(BF16)
            if masked:
                mask = (mask_ref[...] > 0).astype(F32)
                outs[j][PIECE : PIECE + 16, :] = jnp.zeros((16, HD), BF16)
                outs[j][PIECE : PIECE + 16, 0:16] = jnp.broadcast_to(mask, (16, 16)).astype(BF16)


def project(shard, weights, mask):
    state = []
    rounds = gather_rounds(shard)
    for number, given in enumerate(rounds):
        first, last = number == 0, number == len(rounds) - 1
        shards = [(dx, other) for dx, other, _ in given]
        totals = [sds((2, 3, HALF, COLS), F32), sds((8, HALF), F32)]
        extra = mask if last else []
        out_shape = [sds((PIECE + 16 * len(extra), HD), BF16)] * 4 if last else totals
        state = call(
            functools.partial(
                project_kernel, shards=shards, first=first, last=last, masked=bool(extra)
            ),
            out_shape,
            [VM] * (len(state) + len(given) + 2 + len(extra)),
            [VM] * len(out_shape),
            scratch=[pltpu.VMEM(totals[0].shape, F32)] if last else [],
            flops=2 * len(given) * HALF * CHIP * 6 * COLS,
            size=len(given) * CHIP * 6 * COLS * 2,
        )(*state, *[v for _, _, v in given], *weights, *extra)
    return state


def attend_kernel(*refs, offsets, first, last, halves):
    refs = list(refs)
    pieces, mask_refs, other = refs[:4], refs[4:8], refs[8]
    count = len(offsets)
    keys, values = refs[9 : 9 + count], refs[9 + count : 9 + 2 * count]
    refs = refs[9 + 2 * count :]
    if not first:
        top_in, sum_in, total_in = refs[:3]
        refs = refs[3:]
    _, _, _, y, z = place()
    masks = [ref[...].astype(F32)[0:1, :] for ref in mask_refs]
    lane = lax.broadcasted_iota(jnp.int32, (1, HD), 1)
    masks = [
        jnp.broadcast_to(jnp.where(lane < 16, (1.0 - m) * NEG, 0.0), (HALF, HD)).astype(BF16)
        for m in masks
    ]
    group_at = lax.broadcasted_iota(jnp.int32, (QUERIES, HD), 1)
    key_at = lax.broadcasted_iota(jnp.int32, (QUERIES, HD), 0)
    wide = []
    for dy, key in zip(offsets, keys):
        group = lax.rem(y + dy, 4) * 4 + lax.rem(z + turned(key_at // HALF), 4)
        spread = jnp.where(group_at == group, 1.0, 0.0).astype(BF16)
        wide.append(jnp.concatenate([key[...].reshape(QUERIES, HD), spread], axis=1))
    for r in range(2 * QUERIES // CHUNK):
        half = r * CHUNK // QUERIES
        if half not in halves:
            continue
        mine = half == 0
        rows = slice(r * CHUNK, (r + 1) * CHUNK)
        p = r * CHUNK % QUERIES // HALF
        query = [pieces[p + i][0:HALF, :] if mine else other[p + i] for i in range(2)]
        query = [jnp.concatenate([query[i], masks[p + i]], axis=1) for i in range(2)]
        query = jnp.concatenate(query, axis=0)
        scores = [
            lax.dot_general(query, key, (((1,), (1,)), ((), ())), preferred_element_type=F32)
            for key in wide
        ]
        best = functools.reduce(
            jnp.maximum, [s[:, i * HD : (i + 1) * HD] for s in scores for i in range(4)]
        )
        best = jnp.max(best, axis=1, keepdims=True)
        if not first:
            old = top_in[rows, :]
            best = jnp.maximum(best, old[:, 0:1])
            shrink = jnp.exp2(old - best)
            summed, acc = sum_in[rows, :] * shrink, total_in[rows, :] * shrink
        for k, score in enumerate(scores):
            weight = jnp.exp2(score - best)
            parts = sum(weight[:, i * HD : (i + 1) * HD] for i in range(4))
            part = jnp.dot(
                weight.astype(BF16),
                values[k][...].reshape(QUERIES, HD),
                preferred_element_type=F32,
            )
            if first and k == 0:
                summed, acc = parts, part
            else:
                summed, acc = summed + parts, acc + part
        if not last:
            refs[0][rows, :] = jnp.broadcast_to(best, (CHUNK, HD))
            refs[1][rows, :] = summed
            refs[2][rows, :] = acc
            continue
        summed = jnp.sum(summed, axis=1, keepdims=True)
        result = acc / summed
        level = best + jnp.log2(summed)
        rows = slice(r * CHUNK % QUERIES, r * CHUNK % QUERIES + CHUNK)
        out = refs[0]
        out[rows, :] = result
        for i in range(2):
            line = jnp.broadcast_to(level[i * HALF : (i + 1) * HALF, :], (HALF, HD))
            out[QUERIES + p + i : QUERIES + p + i + 1, :] = jnp.transpose(line)[0:1, :]


def attend(pieces, masks, other, blocks, state, half=None):
    offsets = [dy for dy, _, _ in blocks]
    last = half is not None
    out_shape = [sds((QUERIES + 8, HD), F32)] if last else [sds((2 * QUERIES, HD), F32)] * 3
    return call(
        functools.partial(
            attend_kernel,
            offsets=offsets,
            first=not state,
            last=last,
            halves=(half,) if last else (0, 1),
        ),
        out_shape,
        [VM] * (9 + 2 * len(blocks) + len(state)),
        [VM] * len(out_shape),
        limit=16,
        flops=4 * 1024 * 512 * len(blocks) * HD,
        size=MB,
    )(*pieces, *masks, other, *[k for _, k, _ in blocks], *[v for _, _, v in blocks], *state)


def merge_kernel(own, other, *outs):
    for p in range(4):
        rows = slice(p * HALF, (p + 1) * HALF)
        line = slice(QUERIES + p, QUERIES + p + 1)
        gap = jnp.transpose(jnp.broadcast_to(other[line, :] - own[line, :], (HALF, HD)))
        share = 1.0 / (1.0 + jnp.exp2(gap))
        outs[p][...] = (own[rows, :] * share + other[rows, :] * (1.0 - share)).astype(BF16)


def choose_kernel(below, above, out):
    core = place()[2]

    @pl.when(core == 0)
    def _():
        out[...] = below[...]

    @pl.when(core == 1)
    def _():
        out[...] = above[...]


def output_kernel(*refs, shards, first, last, step):
    refs = list(refs)
    if not first:
        total_in = refs[0]
        refs = refs[1:]
    given = refs[: len(shards)]
    weights = refs[len(shards) : len(shards) + 2]
    refs = refs[len(shards) + 2 :]
    if last:
        levels, order, sizes = refs[:3]
        dens, scales, tables = refs[3:5], refs[5:7], refs[7:9]
        outs = refs[9:-1]
    else:
        outs = refs[:-1]
    heads = refs[-1]
    x, l, core, _, z = place()
    starts = []
    for n, ((dx, other), shard) in enumerate(zip(shards, given)):
        starts.append(pl.multiple_of(chip_of(x, l, dx, other) * CHIP_COLS, CHIP_COLS))
        for j in range(4):
            cols = pl.ds(pl.multiple_of(lax.rem(z + (0, 2, 1, 3)[j], 4) * HD, HD), HD)
            heads[n, :, cols] = shard[j]
    for s in range(2):
        acc = None if first else total_in[s]
        for n, start in enumerate(starts):
            part = jnp.dot(
                heads[n], weights[s][pl.ds(start, CHIP_COLS), :], preferred_element_type=F32
            )
            acc = part if acc is None else acc + part
        if not last:
            outs[0][s] = acc
            continue
        denoised = dens[s][...] + sizes[levels[0, step]] * acc
        if step == STEPS - 1:
            outs[s][0] = denoised
            outs[s][1] = acc
        else:
            outs[s][...] = denoised
            features, more = modulated(denoised, levels[0, step + 1], order[0], scales[s], tables[s])
            f = core if s == 0 else 1 - core
            outs[2][pl.ds(pl.multiple_of(f * HALF, HALF), HALF), :] = features
            lanes = more if s == 0 else lanes + more
    if last and step < STEPS - 1:
        store_squares(outs[2], lanes)


def output(attended, weights, step, levels, order, sizes, dens, scales, tables):
    state = []
    rounds = gather_rounds(attended)
    for number, given in enumerate(rounds):
        first, last = number == 0, number == len(rounds) - 1
        shards = [(dx, other) for dx, other, _ in given]
        out_shape, extra, specs = [sds((2, HALF, FEAT), F32)], [], []
        if last:
            if step == STEPS - 1:
                out_shape = [sds((2, HALF, FEAT), F32)] * 2
            else:
                out_shape = [sds((HALF, FEAT), F32)] * 2 + [sds((SHARD, FEAT), BF16)]
            extra = [levels, order, sizes, *dens, *scales, *tables]
            specs = [SM] * 3 + [VM] * 6
        state = call(
            functools.partial(output_kernel, shards=shards, first=first, last=last, step=step),
            out_shape,
            [VM] * (len(state) + len(given) + 2) + specs,
            [VM] * len(out_shape),
            scratch=[pltpu.VMEM((len(given), HALF, CHIP_COLS), BF16)],
            flops=2 * len(given) * HALF * CHIP_COLS * CHIP,
            size=len(given) * CHIP_COLS * CHIP * 2,
        )(*state, *[v for _, _, v in given], *weights, *extra)
    return state


def join_kernel(own, other, denoised, velocity):
    core = place()[2]
    for half, ref in ((core, own), (1 - core, other)):
        rows = pl.ds(pl.multiple_of(half * HALF, HALF), HALF)
        denoised[rows, :] = ref[0]
        velocity[rows, :] = ref[1].astype(BF16)


def body(
    latents,
    input_weights,
    output_weights,
    position_table,
    level_scale,
    step_sizes,
    levels,
    group_order,
    group_mask,
):
    given = (levels, group_order, latents, level_scale, position_table)
    keep, send, keep_latents, send_latents = pl.pallas_call(
        first_kernel,
        out_shape=[sds((ROWS, FEAT), BF16)] * 2 + [sds((HALF, FEAT), F32)] * 2,
        in_specs=[HBM] * 5,
        out_specs=[VM] * 4,
        scratch_shapes=[pltpu.SMEM(v.shape, v.dtype) for v in given[:2]]
        + [pltpu.VMEM(v.shape, v.dtype) for v in given[2:]]
        + [pltpu.SemaphoreType.DMA((5,))],
        compiler_params=pltpu.CompilerParams(vmem_limit_bytes=62 * MB),
    )(*given)
    shard = call(
        pair_kernel,
        sds((SHARD, FEAT), BF16),
        [HBM, VM, HBM],
        VM,
        scratch=[pltpu.VMEM((ROWS, FEAT), BF16), pltpu.SemaphoreType.DMA],
        limit=50,
    )(keep, swap(send), input_weights)
    packed = [send_latents, level_scale, position_table.astype(F32)]
    packed = jnp.concatenate(packed, axis=0)
    in_weights = [input_weights, swap(after(input_weights, shard))]

    for step in range(STEPS):
        sent = project(shard, in_weights, [] if step else [group_mask])
        pieces = [sent[0]] + [move_g(sent[4 - j], Z_MOVES[4 - j]) for j in (1, 2, 3)]
        if step == 0:
            packed = swap(after(packed, sent[0]))
            scales = [level_scale, packed[HALF : HALF + LEVELS]]
            tables = [position_table, packed[HALF + LEVELS :]]
            dens = [keep_latents, packed[:HALF]]
            masks = [v[PIECE:] for v in pieces]
        other = swap(jnp.stack([v[0:HALF] for v in pieces]))
        near = stack([v[HALF:PIECE].reshape(2, HALF, HD) for v in pieces], 1)
        below, above = move_g(near, Y_UP), move_g(near, Y_DOWN)
        state = attend(pieces, masks, other, [(0, near[0], near[1])], [])
        onward = call(choose_kernel, sds(below.shape, BF16), [VM] * 2, VM, limit=4)(below, above)
        far = lax.ppermute(after(onward, *state), ("group", "tensor"), ONWARD)
        blocks = [(3, below[0], below[1]), (1, above[0], above[1])]
        state = attend(pieces, masks, other, blocks, state)
        blocks = [(2, far[0], far[1])]
        theirs = attend(pieces, masks, other, blocks, state, 1)[0]
        mine = attend(pieces, masks, other, blocks, state, 0)[0]
        attended = call(merge_kernel, [sds((HALF, HD), BF16)] * 4, [VM] * 2, [VM] * 4)(
            mine, swap(theirs)
        )
        if step == 0:
            out_weights = [output_weights, swap(after(output_weights, attended[0]))]
        attended = [attended[0]] + [move_g(attended[4 - j], Z_MOVES[4 - j]) for j in (1, 2, 3)]
        result = output(
            stack(attended, 0),
            out_weights,
            step,
            levels,
            group_order,
            step_sizes,
            dens,
            scales,
            tables,
        )
        if step < STEPS - 1:
            dens, shard = result[:2], result[2]
    return tuple(
        call(
            join_kernel,
            [sds((2 * HALF, FEAT), F32), sds((2 * HALF, FEAT), BF16)],
            [VM] * 2,
            [VM] * 2,
        )(result[0], swap(result[1]))
    )


def solution(mesh):
    placed = (
        P("group", "tensor"),
        P(None, None, "tensor"),
        P(None, "tensor"),
        P(None, "tensor"),
        P(None, "tensor"),
        P(),
        P("group", None),
        P("group"),
        P("group", None),
    )
    return jax.shard_map(
        body,
        mesh=mesh,
        in_specs=placed,
        out_specs=(P("group", "tensor"), P("group", "tensor")),
        check_vma=False,
    )
```

```python
import functools
import math

import jax
import jax.numpy as jnp
from jax import lax
from jax.experimental import pallas as pl
from jax.experimental.pallas import tpu as pltpu
from jax.sharding import PartitionSpec as P


D = 6144
HD = 128
STEPS = 2
LEVELS = 32
HALF = 128
FEAT = 384
CHIP = 2 * FEAT
COLS = 256
CHIP_COLS = 2 * COLS
ROWS = HALF + 16
PIECE = 3 * HALF
SHARD = 2 * HALF + 16
NEG = -1e30
F32 = jnp.float32
BF16 = jnp.bfloat16
VM = pl.BlockSpec(memory_space=pltpu.VMEM)
HBM = pl.BlockSpec(memory_space=pltpu.HBM)
SM = pl.BlockSpec(memory_space=pltpu.SMEM)
MB = 1 << 20
QUERIES = 4 * HALF
CHUNK = 256


def t_perm(move):
    pairs = []
    for t in range(16):
        x, l, c = move(t // 4, t // 2 % 2, t % 2)
        pairs.append((t, (x % 4) * 4 + l * 2 + c))
    return pairs


def g_perm(dy, dz):
    return [(g, (g // 4 + dy) % 4 * 4 + (g + dz) % 4) for g in range(16)]


X_UP = t_perm(lambda x, l, c: (x + 1, l, c))
X_DOWN = t_perm(lambda x, l, c: (x - 1, l, c))
X_FAR = t_perm(lambda x, l, c: (x + 2, l, c))
Z_SWAP = t_perm(lambda x, l, c: (x, 1 - l, c))
C_SWAP = t_perm(lambda x, l, c: (x, l, 1 - c))
Y_UP, Y_DOWN = g_perm(1, 0), g_perm(-1, 0)
ONWARD = [
    (g * 16 + t, (Y_DOWN if t % 2 else Y_UP)[g][1] * 16 + t) for g in range(16) for t in range(16)
]
Z_MOVES = {1: g_perm(0, 1), 2: g_perm(0, 2), 3: g_perm(0, -1)}


def move_t(array, pairs):
    return lax.ppermute(array, "tensor", pairs)


def move_g(array, pairs):
    return lax.ppermute(array, "group", pairs)


def swap(array):
    return lax.ppermute(array, "tensor", C_SWAP)


def turned(index):
    return lax.rem(index, 2) * 2 + index // 2


def stack(pieces, axis):
    early = jnp.stack([pieces[0], pieces[2]], axis=axis)
    late = jnp.stack([pieces[1], pieces[3]], axis=axis)
    return jnp.concatenate([after(early), late], axis=axis)


def after(array, *others):
    return lax.optimization_barrier((array, *others))[0]


def sds(shape, dtype):
    return jax.ShapeDtypeStruct(shape, dtype)


def call(kernel, out_shape, in_specs, out_specs, scratch=(), limit=12, flops=0, size=0):
    return pl.pallas_call(
        kernel,
        out_shape=out_shape,
        in_specs=in_specs,
        out_specs=out_specs,
        scratch_shapes=scratch,
        compiler_params=pltpu.CompilerParams(vmem_limit_bytes=limit * MB),
        cost_estimate=pl.CostEstimate(flops=flops, bytes_accessed=size, transcendentals=0),
    )


def place():
    t, g = lax.axis_index("tensor"), lax.axis_index("group")
    return t // 4, t // 2 % 2, t % 2, g // 4, g % 4


def modulated(shifted_from, level, order, scale_ref, table_ref):
    table = table_ref[...].astype(F32)
    row_at = lax.broadcasted_iota(jnp.int32, table.shape, 0)
    position = jnp.sum(jnp.where(row_at == order, table, 0.0), axis=0, keepdims=True)
    shifted = shifted_from + position
    factor = 1.0 + scale_ref[pl.ds(level, 1), :]
    squares = jnp.sum(shifted * shifted, axis=1, keepdims=True)
    return (shifted * factor).astype(BF16), squares


def to_lanes(squares):
    return jnp.transpose(jnp.broadcast_to(squares, (HALF, HALF)))[0:16, :]


def store_squares(out, lanes):
    rows = out.shape[0]
    high = lanes.astype(BF16).astype(F32)
    middle = (lanes - high).astype(BF16).astype(F32)
    low = lanes - high - middle
    at = lax.broadcasted_iota(jnp.int32, lanes.shape, 0)
    parts = jnp.where(at == 0, high, jnp.where(at == 1, middle, jnp.where(at == 2, low, 0.0)))
    out[rows - 16 : rows, 0:HALF] = parts.astype(BF16)
    out[rows - 16 : rows, HALF:FEAT] = jnp.zeros((16, FEAT - HALF), BF16)


def load_squares(ref):
    rows = ref.shape[0]
    return jnp.sum(ref[rows - 16 : rows, 0:HALF].astype(F32), axis=0, keepdims=True)


def first_kernel(*refs):
    sources, outs, held, sems = refs[:5], refs[5:9], refs[9:14], refs[14]
    copies = [
        pltpu.make_async_copy(source, target, sems.at[i])
        for i, (source, target) in enumerate(zip(sources, held))
    ]
    for copy in copies:
        copy.start()
    for copy in copies:
        copy.wait()
    levels, order, latents, scale, table = held
    keep, send, keep_latents, send_latents = outs
    core = place()[2]
    for half, out, out_latents in ((core, keep, keep_latents), (1 - core, send, send_latents)):
        rows = latents[pl.ds(pl.multiple_of(half * HALF, HALF), HALF), :]
        out_latents[...] = rows
        out[0:HALF, :], squares = modulated(rows, levels[0, 0], order[0], scale, table)
        store_squares(out, to_lanes(squares))


def pair_kernel(own_hbm, other, weights, out, own, sem):
    copy = pltpu.make_async_copy(own_hbm, own, sem)
    copy.start()
    copy.wait()
    core = place()[2]
    for f, ref in ((core, own), (1 - core, other)):
        out[pl.ds(pl.multiple_of(f * HALF, HALF), HALF), :] = ref[0:HALF, :]
    store_squares(out, jnp.broadcast_to(load_squares(own) + load_squares(other), (16, HALF)))


def gather_rounds(shard):
    z = move_t(shard, Z_SWAP)
    far = move_t(shard, X_FAR)
    left, right = move_t(shard, X_UP), move_t(shard, X_DOWN)
    z_left, z_right = move_t(z, X_UP), move_t(z, X_DOWN)
    z_far = move_t(far, Z_SWAP)
    return [
        [(0, False, shard), (0, True, z), (3, False, left), (1, False, right)],
        [(2, False, far), (3, True, z_left), (1, True, z_right)],
        [(2, True, z_far)],
    ]


def chip_of(x, l, dx, other):
    return lax.rem(x + dx, 4) * 2 + (1 - l if other else l)


def project_kernel(*refs, shards, first, last, masked):
    refs = list(refs)
    total_in = square_in = None
    if not first:
        total_in, square_in = refs[:2]
        refs = refs[2:]
    given = refs[: len(shards)]
    weights = refs[len(shards) : len(shards) + 2]
    outs = refs[len(shards) + 2 :]
    if masked:
        mask_ref, outs = outs[0], outs[1:]
    x, l, core, _, z = place()
    lhs, starts = [], []
    square = jnp.zeros((8, HALF), F32) if first else square_in[...]
    for (dx, other), shard in zip(shards, given):
        lhs.append(jnp.concatenate([shard[0:HALF, :], shard[HALF : 2 * HALF, :]], axis=1))
        starts.append(pl.multiple_of(chip_of(x, l, dx, other) * CHIP, CHIP))
        square = square + jnp.broadcast_to(load_squares(shard), square.shape)
    if last:
        total = outs[4]
        rstd = lax.rsqrt(square[0:1, :] / D + 1e-06)
        rstd = jnp.transpose(jnp.broadcast_to(rstd, (HALF, HALF)))
        rstd = jnp.concatenate([rstd, rstd], axis=1)
    else:
        total = outs[0]
        outs[1][...] = square
    for s in range(2):
        for i in range(3):
            acc = None if first else total_in[s, i]
            for row, start in zip(lhs, starts):
                part = jnp.dot(row, weights[s][i, pl.ds(start, CHIP), :], preferred_element_type=F32)
                acc = part if acc is None else acc + part
            if last:
                acc = acc * rstd
                if i == 0:
                    acc = acc * (math.log2(math.e) / math.sqrt(HD))
            total[s, i] = acc
    if last:
        for j in range(4):
            head = lax.rem(z + j, 4)
            which = jnp.where(head // 2 == core, 0, 1)
            cols = pl.ds(pl.multiple_of(lax.rem(head, 2) * HD, HD), HD)
            for i in range(3):
                outs[j][i * HALF : (i + 1) * HALF, :] = total[which, i, :, cols].astype(BF16)
            if masked:
                mask = (mask_ref[...] > 0).astype(F32)
                outs[j][PIECE : PIECE + 16, :] = jnp.zeros((16, HD), BF16)
                outs[j][PIECE : PIECE + 16, 0:16] = jnp.broadcast_to(mask, (16, 16)).astype(BF16)


def project(shard, weights, mask):
    state = []
    rounds = gather_rounds(shard)
    for number, given in enumerate(rounds):
        first, last = number == 0, number == len(rounds) - 1
        shards = [(dx, other) for dx, other, _ in given]
        totals = [sds((2, 3, HALF, COLS), F32), sds((8, HALF), F32)]
        extra = mask if last else []
        out_shape = [sds((PIECE + 16 * len(extra), HD), BF16)] * 4 if last else totals
        state = call(
            functools.partial(
                project_kernel, shards=shards, first=first, last=last, masked=bool(extra)
            ),
            out_shape,
            [VM] * (len(state) + len(given) + 2 + len(extra)),
            [VM] * len(out_shape),
            scratch=[pltpu.VMEM(totals[0].shape, F32)] if last else [],
            flops=2 * len(given) * HALF * CHIP * 6 * COLS,
            size=len(given) * CHIP * 6 * COLS * 2,
        )(*state, *[v for _, _, v in given], *weights, *extra)
    return state


def attend_kernel(*refs, offsets, first, last, halves):
    refs = list(refs)
    pieces, mask_refs, other = refs[:4], refs[4:8], refs[8]
    count = len(offsets)
    keys, values = refs[9 : 9 + count], refs[9 + count : 9 + 2 * count]
    refs = refs[9 + 2 * count :]
    if not first:
        top_in, sum_in, total_in = refs[:3]
        refs = refs[3:]
    _, _, _, y, z = place()
    masks = [ref[...].astype(F32)[0:1, :] for ref in mask_refs]
    lane = lax.broadcasted_iota(jnp.int32, (1, HD), 1)
    masks = [
        jnp.broadcast_to(jnp.where(lane < 16, (1.0 - m) * NEG, 0.0), (HALF, HD)).astype(BF16)
        for m in masks
    ]
    group_at = lax.broadcasted_iota(jnp.int32, (QUERIES, HD), 1)
    key_at = lax.broadcasted_iota(jnp.int32, (QUERIES, HD), 0)
    wide = []
    for dy, key in zip(offsets, keys):
        group = lax.rem(y + dy, 4) * 4 + lax.rem(z + turned(key_at // HALF), 4)
        spread = jnp.where(group_at == group, 1.0, 0.0).astype(BF16)
        wide.append(jnp.concatenate([key[...].reshape(QUERIES, HD), spread], axis=1))
    for r in range(2 * QUERIES // CHUNK):
        half = r * CHUNK // QUERIES
        if half not in halves:
            continue
        mine = half == 0
        rows = slice(r * CHUNK, (r + 1) * CHUNK)
        p = r * CHUNK % QUERIES // HALF
        query = [pieces[p + i][0:HALF, :] if mine else other[p + i] for i in range(2)]
        query = [jnp.concatenate([query[i], masks[p + i]], axis=1) for i in range(2)]
        query = jnp.concatenate(query, axis=0)
        scores = [
            lax.dot_general(query, key, (((1,), (1,)), ((), ())), preferred_element_type=F32)
            for key in wide
        ]
        best = functools.reduce(
            jnp.maximum, [s[:, i * HD : (i + 1) * HD] for s in scores for i in range(4)]
        )
        best = jnp.max(best, axis=1, keepdims=True)
        if not first:
            old = top_in[rows, :]
            best = jnp.maximum(best, old[:, 0:1])
            shrink = jnp.exp2(old - best)
            summed, acc = sum_in[rows, :] * shrink, total_in[rows, :] * shrink
        for k, score in enumerate(scores):
            weight = jnp.exp2(score - best)
            parts = sum(weight[:, i * HD : (i + 1) * HD] for i in range(4))
            part = jnp.dot(
                weight.astype(BF16),
                values[k][...].reshape(QUERIES, HD),
                preferred_element_type=F32,
            )
            if first and k == 0:
                summed, acc = parts, part
            else:
                summed, acc = summed + parts, acc + part
        if not last:
            refs[0][rows, :] = jnp.broadcast_to(best, (CHUNK, HD))
            refs[1][rows, :] = summed
            refs[2][rows, :] = acc
            continue
        summed = jnp.sum(summed, axis=1, keepdims=True)
        result = acc / summed
        level = best + jnp.log2(summed)
        rows = slice(r * CHUNK % QUERIES, r * CHUNK % QUERIES + CHUNK)
        out = refs[0]
        out[rows, :] = result
        for i in range(2):
            line = jnp.broadcast_to(level[i * HALF : (i + 1) * HALF, :], (HALF, HD))
            out[QUERIES + p + i : QUERIES + p + i + 1, :] = jnp.transpose(line)[0:1, :]


def attend(pieces, masks, other, blocks, state, half=None):
    offsets = [dy for dy, _, _ in blocks]
    last = half is not None
    out_shape = [sds((QUERIES + 8, HD), F32)] if last else [sds((2 * QUERIES, HD), F32)] * 3
    return call(
        functools.partial(
            attend_kernel,
            offsets=offsets,
            first=not state,
            last=last,
            halves=(half,) if last else (0, 1),
        ),
        out_shape,
        [VM] * (9 + 2 * len(blocks) + len(state)),
        [VM] * len(out_shape),
        limit=16,
        flops=4 * 1024 * 512 * len(blocks) * HD,
        size=MB,
    )(*pieces, *masks, other, *[k for _, k, _ in blocks], *[v for _, _, v in blocks], *state)


def merge_kernel(own, other, *outs):
    for p in range(4):
        rows = slice(p * HALF, (p + 1) * HALF)
        line = slice(QUERIES + p, QUERIES + p + 1)
        gap = jnp.transpose(jnp.broadcast_to(other[line, :] - own[line, :], (HALF, HD)))
        share = 1.0 / (1.0 + jnp.exp2(gap))
        outs[p][...] = (own[rows, :] * share + other[rows, :] * (1.0 - share)).astype(BF16)


def choose_kernel(below, above, out):
    core = place()[2]

    @pl.when(core == 0)
    def _():
        out[...] = below[...]

    @pl.when(core == 1)
    def _():
        out[...] = above[...]


def output_kernel(*refs, shards, first, last, step, sets):
    refs = list(refs)
    if not first:
        total_in = refs[0]
        refs = refs[1:]
    given = refs[: len(shards)]
    weights = refs[len(shards) : len(shards) + 2]
    refs = refs[len(shards) + 2 :]
    if last:
        levels, order, sizes = refs[:3]
        dens, scales, tables = refs[3:5], refs[5:7], refs[7:9]
        outs = refs[9:-1]
    else:
        outs = refs[:-1]
    heads = refs[-1]
    x, l, core, _, z = place()
    starts = []
    for n, ((dx, other), shard) in enumerate(zip(shards, given)):
        starts.append(pl.multiple_of(chip_of(x, l, dx, other) * CHIP_COLS, CHIP_COLS))
        for j in range(4):
            cols = pl.ds(pl.multiple_of(lax.rem(z + (0, 2, 1, 3)[j], 4) * HD, HD), HD)
            heads[n, :, cols] = shard[j]
    for s in sets:
        acc = None if first else total_in[s]
        for n, start in enumerate(starts):
            part = jnp.dot(
                heads[n], weights[s][pl.ds(start, CHIP_COLS), :], preferred_element_type=F32
            )
            acc = part if acc is None else acc + part
        if not last:
            outs[0][s] = acc
            continue
        denoised = dens[s][...] + sizes[levels[0, step]] * acc
        if step == STEPS - 1:
            outs[0][0] = denoised
            outs[0][1] = acc
        else:
            outs[s][...] = denoised
            features, more = modulated(denoised, levels[0, step + 1], order[0], scales[s], tables[s])
            f = core if s == 0 else 1 - core
            outs[2][pl.ds(pl.multiple_of(f * HALF, HALF), HALF), :] = features
            squares = more if s == 0 else squares + more
    if last and step < STEPS - 1:
        store_squares(outs[2], to_lanes(squares))


def output(attended, weights, step, levels, order, sizes, dens, scales, tables):
    state = []
    rounds = gather_rounds(attended)
    for number, given in enumerate(rounds):
        first, last = number == 0, number == len(rounds) - 1
        shards = [(dx, other) for dx, other, _ in given]
        out_shape, extra, specs = [sds((2, HALF, FEAT), F32)], [], []
        parts = [(0, 1)]
        if last:
            if step == STEPS - 1:
                parts = [(1,), (0,)]
            else:
                out_shape = [sds((HALF, FEAT), F32)] * 2 + [sds((SHARD, FEAT), BF16)]
            extra = [levels, order, sizes, *dens, *scales, *tables]
            specs = [SM] * 3 + [VM] * 6
        given_state, state = state, []
        for sets in parts:
            state += call(
                functools.partial(
                    output_kernel, shards=shards, first=first, last=last, step=step, sets=sets
                ),
                out_shape,
                [VM] * (len(given_state) + len(given) + 2) + specs,
                [VM] * len(out_shape),
                scratch=[pltpu.VMEM((len(given), HALF, CHIP_COLS), BF16)],
                flops=len(sets) * len(given) * HALF * CHIP_COLS * CHIP,
                size=len(given) * CHIP_COLS * CHIP * 2,
            )(*given_state, *[v for _, _, v in given], *weights, *extra)
    return state


def join_kernel(own, other, denoised, velocity):
    core = place()[2]
    for half, ref in ((core, own), (1 - core, other)):
        rows = pl.ds(pl.multiple_of(half * HALF, HALF), HALF)
        denoised[rows, :] = ref[0]
        velocity[rows, :] = ref[1].astype(BF16)


def body(
    latents,
    input_weights,
    output_weights,
    position_table,
    level_scale,
    step_sizes,
    levels,
    group_order,
    group_mask,
):
    given = (levels, group_order, latents, level_scale, position_table)
    keep, send, keep_latents, send_latents = pl.pallas_call(
        first_kernel,
        out_shape=[sds((ROWS, FEAT), BF16)] * 2 + [sds((HALF, FEAT), F32)] * 2,
        in_specs=[HBM] * 5,
        out_specs=[VM] * 4,
        scratch_shapes=[pltpu.SMEM(v.shape, v.dtype) for v in given[:2]]
        + [pltpu.VMEM(v.shape, v.dtype) for v in given[2:]]
        + [pltpu.SemaphoreType.DMA((5,))],
        compiler_params=pltpu.CompilerParams(vmem_limit_bytes=62 * MB),
    )(*given)
    shard = call(
        pair_kernel,
        sds((SHARD, FEAT), BF16),
        [HBM, VM, HBM],
        VM,
        scratch=[pltpu.VMEM((ROWS, FEAT), BF16), pltpu.SemaphoreType.DMA],
        limit=50,
    )(keep, swap(send), input_weights)
    packed = [send_latents, level_scale, position_table.astype(F32)]
    packed = jnp.concatenate(packed, axis=0)
    in_weights = [input_weights, swap(after(input_weights, shard))]

    for step in range(STEPS):
        sent = project(shard, in_weights, [] if step else [group_mask])
        pieces = [sent[0]] + [move_g(sent[4 - j], Z_MOVES[4 - j]) for j in (1, 2, 3)]
        if step == 0:
            packed = swap(after(packed, sent[0]))
            scales = [level_scale, packed[HALF : HALF + LEVELS]]
            tables = [position_table, packed[HALF + LEVELS :]]
            dens = [keep_latents, packed[:HALF]]
            masks = [v[PIECE:] for v in pieces]
        other = swap(jnp.stack([v[0:HALF] for v in pieces]))
        near = stack([v[HALF:PIECE].reshape(2, HALF, HD) for v in pieces], 1)
        below, above = move_g(near, Y_UP), move_g(near, Y_DOWN)
        state = attend(pieces, masks, other, [(0, near[0], near[1])], [])
        onward = call(choose_kernel, sds(below.shape, BF16), [VM] * 2, VM, limit=4)(below, above)
        far = lax.ppermute(after(onward, *state), ("group", "tensor"), ONWARD)
        blocks = [(3, below[0], below[1]), (1, above[0], above[1])]
        state = attend(pieces, masks, other, blocks, state)
        blocks = [(2, far[0], far[1])]
        theirs = attend(pieces, masks, other, blocks, state, 1)[0]
        mine = attend(pieces, masks, other, blocks, state, 0)[0]
        attended = call(merge_kernel, [sds((HALF, HD), BF16)] * 4, [VM] * 2, [VM] * 4)(
            mine, swap(theirs)
        )
        if step == 0:
            out_weights = [output_weights, swap(after(output_weights, attended[0]))]
        attended = [attended[0]] + [move_g(attended[4 - j], Z_MOVES[4 - j]) for j in (1, 2, 3)]
        result = output(
            stack(attended, 0),
            out_weights,
            step,
            levels,
            group_order,
            step_sizes,
            dens,
            scales,
            tables,
        )
        if step < STEPS - 1:
            dens, shard = result[:2], result[2]
    return tuple(
        call(
            join_kernel,
            [sds((2 * HALF, FEAT), F32), sds((2 * HALF, FEAT), BF16)],
            [VM] * 2,
            [VM] * 2,
        )(result[1], swap(result[0]))
    )


def solution(mesh):
    placed = (
        P("group", "tensor"),
        P(None, None, "tensor"),
        P(None, "tensor"),
        P(None, "tensor"),
        P(None, "tensor"),
        P(),
        P("group", None),
        P("group"),
        P("group", None),
    )
    return jax.shard_map(
        body,
        mesh=mesh,
        in_specs=placed,
        out_specs=(P("group", "tensor"), P("group", "tensor")),
        check_vma=False,
    )
```

```python
import functools
import math

import jax
import jax.numpy as jnp
from jax import lax
from jax.experimental import pallas as pl
from jax.experimental.pallas import tpu as pltpu
from jax.sharding import PartitionSpec as P


D = 6144
HD = 128
STEPS = 2
LEVELS = 32
HALF = 128
FEAT = 384
CHIP = 2 * FEAT
COLS = 256
CHIP_COLS = 2 * COLS
ROWS = HALF + 16
PIECE = 3 * HALF
SHARD = 2 * HALF + 16
NEG = -1e30
F32 = jnp.float32
BF16 = jnp.bfloat16
VM = pl.BlockSpec(memory_space=pltpu.VMEM)
HBM = pl.BlockSpec(memory_space=pltpu.HBM)
SM = pl.BlockSpec(memory_space=pltpu.SMEM)
MB = 1 << 20
QUERIES = 4 * HALF
CHUNK = 512


def t_perm(move):
    pairs = []
    for t in range(16):
        x, l, c = move(t // 4, t // 2 % 2, t % 2)
        pairs.append((t, (x % 4) * 4 + l * 2 + c))
    return pairs


def g_perm(dy, dz):
    return [(g, (g // 4 + dy) % 4 * 4 + (g + dz) % 4) for g in range(16)]


X_UP = t_perm(lambda x, l, c: (x + 1, l, c))
X_DOWN = t_perm(lambda x, l, c: (x - 1, l, c))
X_FAR = t_perm(lambda x, l, c: (x + 2, l, c))
Z_SWAP = t_perm(lambda x, l, c: (x, 1 - l, c))
C_SWAP = t_perm(lambda x, l, c: (x, l, 1 - c))
Y_UP, Y_DOWN = g_perm(1, 0), g_perm(-1, 0)
ONWARD = [
    (g * 16 + t, (Y_DOWN if t % 2 else Y_UP)[g][1] * 16 + t) for g in range(16) for t in range(16)
]
Z_MOVES = {1: g_perm(0, 1), 2: g_perm(0, 2), 3: g_perm(0, -1)}


def move_t(array, pairs):
    return lax.ppermute(array, "tensor", pairs)


def move_g(array, pairs):
    return lax.ppermute(array, "group", pairs)


def swap(array):
    return lax.ppermute(array, "tensor", C_SWAP)


def turned(index):
    return lax.rem(index, 2) * 2 + index // 2


def stack(pieces, axis):
    early = jnp.stack([pieces[0], pieces[2]], axis=axis)
    late = jnp.stack([pieces[1], pieces[3]], axis=axis)
    return jnp.concatenate([after(early), late], axis=axis)


def after(array, *others):
    return lax.optimization_barrier((array, *others))[0]


def sds(shape, dtype):
    return jax.ShapeDtypeStruct(shape, dtype)


def call(kernel, out_shape, in_specs, out_specs, scratch=(), limit=12, flops=0, size=0):
    return pl.pallas_call(
        kernel,
        out_shape=out_shape,
        in_specs=in_specs,
        out_specs=out_specs,
        scratch_shapes=scratch,
        compiler_params=pltpu.CompilerParams(vmem_limit_bytes=limit * MB),
        cost_estimate=pl.CostEstimate(flops=flops, bytes_accessed=size, transcendentals=0),
    )


def place():
    t, g = lax.axis_index("tensor"), lax.axis_index("group")
    return t // 4, t // 2 % 2, t % 2, g // 4, g % 4


def modulated(shifted_from, level, order, scale_ref, table_ref):
    table = table_ref[...].astype(F32)
    row_at = lax.broadcasted_iota(jnp.int32, table.shape, 0)
    position = jnp.sum(jnp.where(row_at == order, table, 0.0), axis=0, keepdims=True)
    shifted = shifted_from + position
    factor = 1.0 + scale_ref[pl.ds(level, 1), :]
    squares = jnp.sum(shifted * shifted, axis=1, keepdims=True)
    return (shifted * factor).astype(BF16), squares


def to_lanes(squares):
    return jnp.transpose(jnp.broadcast_to(squares, (HALF, HALF)))[0:16, :]


def store_squares(out, lanes):
    rows = out.shape[0]
    high = lanes.astype(BF16).astype(F32)
    middle = (lanes - high).astype(BF16).astype(F32)
    low = lanes - high - middle
    at = lax.broadcasted_iota(jnp.int32, lanes.shape, 0)
    parts = jnp.where(at == 0, high, jnp.where(at == 1, middle, jnp.where(at == 2, low, 0.0)))
    out[rows - 16 : rows, 0:HALF] = parts.astype(BF16)
    out[rows - 16 : rows, HALF:FEAT] = jnp.zeros((16, FEAT - HALF), BF16)


def load_squares(ref):
    rows = ref.shape[0]
    return jnp.sum(ref[rows - 16 : rows, 0:HALF].astype(F32), axis=0, keepdims=True)


def first_kernel(*refs):
    sources, outs, held, sems = refs[:5], refs[5:9], refs[9:14], refs[14]
    copies = [
        pltpu.make_async_copy(source, target, sems.at[i])
        for i, (source, target) in enumerate(zip(sources, held))
    ]
    for copy in copies:
        copy.start()
    for copy in copies:
        copy.wait()
    levels, order, latents, scale, table = held
    keep, send, keep_latents, send_latents = outs
    core = place()[2]
    for half, out, out_latents in ((core, keep, keep_latents), (1 - core, send, send_latents)):
        rows = latents[pl.ds(pl.multiple_of(half * HALF, HALF), HALF), :]
        out_latents[...] = rows
        out[0:HALF, :], squares = modulated(rows, levels[0, 0], order[0], scale, table)
        store_squares(out, to_lanes(squares))


def pair_kernel(own_hbm, other, weights, out, own, sem):
    copy = pltpu.make_async_copy(own_hbm, own, sem)
    copy.start()
    copy.wait()
    core = place()[2]
    for f, ref in ((core, own), (1 - core, other)):
        out[pl.ds(pl.multiple_of(f * HALF, HALF), HALF), :] = ref[0:HALF, :]
    store_squares(out, jnp.broadcast_to(load_squares(own) + load_squares(other), (16, HALF)))


def gather_rounds(shard):
    z = move_t(shard, Z_SWAP)
    far = move_t(shard, X_FAR)
    left, right = move_t(shard, X_UP), move_t(shard, X_DOWN)
    z_left, z_right = move_t(z, X_UP), move_t(z, X_DOWN)
    z_far = move_t(far, Z_SWAP)
    return [
        [(0, False, shard), (0, True, z), (3, False, left), (1, False, right)],
        [(2, False, far), (3, True, z_left), (1, True, z_right)],
        [(2, True, z_far)],
    ]


def chip_of(x, l, dx, other):
    return lax.rem(x + dx, 4) * 2 + (1 - l if other else l)


def project_kernel(*refs, shards, first, last, masked):
    refs = list(refs)
    total_in = square_in = None
    if not first:
        total_in, square_in = refs[:2]
        refs = refs[2:]
    given = refs[: len(shards)]
    weights = refs[len(shards) : len(shards) + 2]
    outs = refs[len(shards) + 2 :]
    if masked:
        mask_ref, outs = outs[0], outs[1:]
    x, l, core, _, z = place()
    lhs, starts = [], []
    square = jnp.zeros((8, HALF), F32) if first else square_in[...]
    for (dx, other), shard in zip(shards, given):
        lhs.append(jnp.concatenate([shard[0:HALF, :], shard[HALF : 2 * HALF, :]], axis=1))
        starts.append(pl.multiple_of(chip_of(x, l, dx, other) * CHIP, CHIP))
        square = square + jnp.broadcast_to(load_squares(shard), square.shape)
    if last:
        total = outs[4]
        rstd = lax.rsqrt(square[0:1, :] / D + 1e-06)
        rstd = jnp.transpose(jnp.broadcast_to(rstd, (HALF, HALF)))
        rstd = jnp.concatenate([rstd, rstd], axis=1)
    else:
        total = outs[0]
        outs[1][...] = square
    for s in range(2):
        for i in range(3):
            acc = None if first else total_in[s, i]
            for row, start in zip(lhs, starts):
                part = jnp.dot(row, weights[s][i, pl.ds(start, CHIP), :], preferred_element_type=F32)
                acc = part if acc is None else acc + part
            if last:
                acc = acc * rstd
                if i == 0:
                    acc = acc * (math.log2(math.e) / math.sqrt(HD))
            total[s, i] = acc
    if last:
        for j in range(4):
            head = lax.rem(z + j, 4)
            which = jnp.where(head // 2 == core, 0, 1)
            cols = pl.ds(pl.multiple_of(lax.rem(head, 2) * HD, HD), HD)
            for i in range(3):
                outs[j][i * HALF : (i + 1) * HALF, :] = total[which, i, :, cols].astype(BF16)
            if masked:
                mask = (mask_ref[...] > 0).astype(F32)
                outs[j][PIECE : PIECE + 16, :] = jnp.zeros((16, HD), BF16)
                outs[j][PIECE : PIECE + 16, 0:16] = jnp.broadcast_to(mask, (16, 16)).astype(BF16)


def project(shard, weights, mask):
    state = []
    rounds = gather_rounds(shard)
    for number, given in enumerate(rounds):
        first, last = number == 0, number == len(rounds) - 1
        shards = [(dx, other) for dx, other, _ in given]
        totals = [sds((2, 3, HALF, COLS), F32), sds((8, HALF), F32)]
        extra = mask if last else []
        out_shape = [sds((PIECE + 16 * len(extra), HD), BF16)] * 4 if last else totals
        state = call(
            functools.partial(
                project_kernel, shards=shards, first=first, last=last, masked=bool(extra)
            ),
            out_shape,
            [VM] * (len(state) + len(given) + 2 + len(extra)),
            [VM] * len(out_shape),
            scratch=[pltpu.VMEM(totals[0].shape, F32)] if last else [],
            flops=2 * len(given) * HALF * CHIP * 6 * COLS,
            size=len(given) * CHIP * 6 * COLS * 2,
        )(*state, *[v for _, _, v in given], *weights, *extra)
    return state


def attend_kernel(*refs, offsets, first, last, halves):
    refs = list(refs)
    pieces, mask_refs, other = refs[:4], refs[4:8], refs[8]
    count = len(offsets)
    keys, values = refs[9 : 9 + count], refs[9 + count : 9 + 2 * count]
    refs = refs[9 + 2 * count :]
    if not first:
        top_in, sum_in, total_in = refs[:3]
        refs = refs[3:]
    _, _, _, y, z = place()
    masks = [ref[...].astype(F32)[0:1, :] for ref in mask_refs]
    lane = lax.broadcasted_iota(jnp.int32, (1, HD), 1)
    masks = [
        jnp.broadcast_to(jnp.where(lane < 16, (1.0 - m) * NEG, 0.0), (HALF, HD)).astype(BF16)
        for m in masks
    ]
    group_at = lax.broadcasted_iota(jnp.int32, (QUERIES, HD), 1)
    key_at = lax.broadcasted_iota(jnp.int32, (QUERIES, HD), 0)
    wide = []
    for dy, key in zip(offsets, keys):
        group = lax.rem(y + dy, 4) * 4 + lax.rem(z + turned(key_at // HALF), 4)
        spread = jnp.where(group_at == group, 1.0, 0.0).astype(BF16)
        wide.append(jnp.concatenate([key[...].reshape(QUERIES, HD), spread], axis=1))
    for r in range(2 * QUERIES // CHUNK):
        half = r * CHUNK // QUERIES
        if half not in halves:
            continue
        mine = half == 0
        rows = slice(r * CHUNK, (r + 1) * CHUNK)
        p = r * CHUNK % QUERIES // HALF
        query = [pieces[p + i][0:HALF, :] if mine else other[p + i] for i in range(CHUNK // HALF)]
        query = [jnp.concatenate([query[i], masks[p + i]], axis=1) for i in range(CHUNK // HALF)]
        query = jnp.concatenate(query, axis=0)
        scores = [
            lax.dot_general(query, key, (((1,), (1,)), ((), ())), preferred_element_type=F32)
            for key in wide
        ]
        best = functools.reduce(
            jnp.maximum, [s[:, i * HD : (i + 1) * HD] for s in scores for i in range(4)]
        )
        best = jnp.max(best, axis=1, keepdims=True)
        if not first:
            old = top_in[rows, :]
            best = jnp.maximum(best, old[:, 0:1])
            shrink = jnp.exp2(old - best)
            summed, acc = sum_in[rows, :] * shrink, total_in[rows, :] * shrink
        for k, score in enumerate(scores):
            weight = jnp.exp2(score - best)
            parts = sum(weight[:, i * HD : (i + 1) * HD] for i in range(4))
            part = jnp.dot(
                weight.astype(BF16),
                values[k][...].reshape(QUERIES, HD),
                preferred_element_type=F32,
            )
            if first and k == 0:
                summed, acc = parts, part
            else:
                summed, acc = summed + parts, acc + part
        if not last:
            refs[0][rows, :] = jnp.broadcast_to(best, (CHUNK, HD))
            refs[1][rows, :] = summed
            refs[2][rows, :] = acc
            continue
        summed = jnp.sum(summed, axis=1, keepdims=True)
        result = acc / summed
        level = best + jnp.log2(summed)
        rows = slice(r * CHUNK % QUERIES, r * CHUNK % QUERIES + CHUNK)
        out = refs[0]
        out[rows, :] = result
        for i in range(CHUNK // HALF):
            line = jnp.broadcast_to(level[i * HALF : (i + 1) * HALF, :], (HALF, HD))
            out[QUERIES + p + i : QUERIES + p + i + 1, :] = jnp.transpose(line)[0:1, :]


def attend(pieces, masks, other, blocks, state, half=None):
    offsets = [dy for dy, _, _ in blocks]
    last = half is not None
    out_shape = [sds((QUERIES + 8, HD), F32)] if last else [sds((2 * QUERIES, HD), F32)] * 3
    return call(
        functools.partial(
            attend_kernel,
            offsets=offsets,
            first=not state,
            last=last,
            halves=(half,) if last else (0, 1),
        ),
        out_shape,
        [VM] * (9 + 2 * len(blocks) + len(state)),
        [VM] * len(out_shape),
        limit=16,
        flops=4 * 1024 * 512 * len(blocks) * HD,
        size=MB,
    )(*pieces, *masks, other, *[k for _, k, _ in blocks], *[v for _, _, v in blocks], *state)


def merge_kernel(own, other, *outs):
    for p in range(4):
        rows = slice(p * HALF, (p + 1) * HALF)
        line = slice(QUERIES + p, QUERIES + p + 1)
        gap = jnp.transpose(jnp.broadcast_to(other[line, :] - own[line, :], (HALF, HD)))
        share = 1.0 / (1.0 + jnp.exp2(gap))
        outs[p][...] = (own[rows, :] * share + other[rows, :] * (1.0 - share)).astype(BF16)


def choose_kernel(below, above, out):
    core = place()[2]

    @pl.when(core == 0)
    def _():
        out[...] = below[...]

    @pl.when(core == 1)
    def _():
        out[...] = above[...]


def output_kernel(*refs, shards, first, last, step, sets):
    refs = list(refs)
    if not first:
        total_in = refs[0]
        refs = refs[1:]
    given = refs[: len(shards)]
    weights = refs[len(shards) : len(shards) + 2]
    refs = refs[len(shards) + 2 :]
    if last:
        levels, order, sizes = refs[:3]
        dens, scales, tables = refs[3:5], refs[5:7], refs[7:9]
        outs = refs[9:-1]
    else:
        outs = refs[:-1]
    heads = refs[-1]
    x, l, core, _, z = place()
    starts = []
    for n, ((dx, other), shard) in enumerate(zip(shards, given)):
        starts.append(pl.multiple_of(chip_of(x, l, dx, other) * CHIP_COLS, CHIP_COLS))
        for j in range(4):
            cols = pl.ds(pl.multiple_of(lax.rem(z + (0, 2, 1, 3)[j], 4) * HD, HD), HD)
            heads[n, :, cols] = shard[j]
    for s in sets:
        acc = None if first else total_in[s]
        for n, start in enumerate(starts):
            part = jnp.dot(
                heads[n], weights[s][pl.ds(start, CHIP_COLS), :], preferred_element_type=F32
            )
            acc = part if acc is None else acc + part
        if not last:
            outs[0][s] = acc
            continue
        denoised = dens[s][...] + sizes[levels[0, step]] * acc
        if step == STEPS - 1:
            outs[0][0] = denoised
            outs[0][1] = acc
        else:
            outs[s][...] = denoised
            features, more = modulated(denoised, levels[0, step + 1], order[0], scales[s], tables[s])
            f = core if s == 0 else 1 - core
            outs[2][pl.ds(pl.multiple_of(f * HALF, HALF), HALF), :] = features
            squares = more if s == 0 else squares + more
    if last and step < STEPS - 1:
        store_squares(outs[2], to_lanes(squares))


def output(attended, weights, step, levels, order, sizes, dens, scales, tables):
    state = []
    rounds = gather_rounds(attended)
    for number, given in enumerate(rounds):
        first, last = number == 0, number == len(rounds) - 1
        shards = [(dx, other) for dx, other, _ in given]
        out_shape, extra, specs = [sds((2, HALF, FEAT), F32)], [], []
        parts = [(0, 1)]
        if last:
            if step == STEPS - 1:
                parts = [(1,), (0,)]
            else:
                out_shape = [sds((HALF, FEAT), F32)] * 2 + [sds((SHARD, FEAT), BF16)]
            extra = [levels, order, sizes, *dens, *scales, *tables]
            specs = [SM] * 3 + [VM] * 6
        given_state, state = state, []
        for sets in parts:
            state += call(
                functools.partial(
                    output_kernel, shards=shards, first=first, last=last, step=step, sets=sets
                ),
                out_shape,
                [VM] * (len(given_state) + len(given) + 2) + specs,
                [VM] * len(out_shape),
                scratch=[pltpu.VMEM((len(given), HALF, CHIP_COLS), BF16)],
                flops=len(sets) * len(given) * HALF * CHIP_COLS * CHIP,
                size=len(given) * CHIP_COLS * CHIP * 2,
            )(*given_state, *[v for _, _, v in given], *weights, *extra)
    return state


def join_kernel(own, other, denoised, velocity):
    core = place()[2]
    for half, ref in ((core, own), (1 - core, other)):
        rows = pl.ds(pl.multiple_of(half * HALF, HALF), HALF)
        denoised[rows, :] = ref[0]
        velocity[rows, :] = ref[1].astype(BF16)


def body(
    latents,
    input_weights,
    output_weights,
    position_table,
    level_scale,
    step_sizes,
    levels,
    group_order,
    group_mask,
):
    given = (levels, group_order, latents, level_scale, position_table)
    keep, send, keep_latents, send_latents = pl.pallas_call(
        first_kernel,
        out_shape=[sds((ROWS, FEAT), BF16)] * 2 + [sds((HALF, FEAT), F32)] * 2,
        in_specs=[HBM] * 5,
        out_specs=[VM] * 4,
        scratch_shapes=[pltpu.SMEM(v.shape, v.dtype) for v in given[:2]]
        + [pltpu.VMEM(v.shape, v.dtype) for v in given[2:]]
        + [pltpu.SemaphoreType.DMA((5,))],
        compiler_params=pltpu.CompilerParams(vmem_limit_bytes=62 * MB),
    )(*given)
    shard = call(
        pair_kernel,
        sds((SHARD, FEAT), BF16),
        [HBM, VM, HBM],
        VM,
        scratch=[pltpu.VMEM((ROWS, FEAT), BF16), pltpu.SemaphoreType.DMA],
        limit=50,
    )(keep, swap(send), input_weights)
    packed = [send_latents, level_scale, position_table.astype(F32)]
    packed = jnp.concatenate(packed, axis=0)
    in_weights = [input_weights, swap(after(input_weights, shard))]

    for step in range(STEPS):
        sent = project(shard, in_weights, [] if step else [group_mask])
        pieces = [sent[0]] + [move_g(sent[4 - j], Z_MOVES[4 - j]) for j in (1, 2, 3)]
        if step == 0:
            packed = swap(after(packed, sent[0]))
            scales = [level_scale, packed[HALF : HALF + LEVELS]]
            tables = [position_table, packed[HALF + LEVELS :]]
            dens = [keep_latents, packed[:HALF]]
            masks = [v[PIECE:] for v in pieces]
        other = swap(jnp.stack([v[0:HALF] for v in pieces]))
        near = stack([v[HALF:PIECE].reshape(2, HALF, HD) for v in pieces], 1)
        below, above = move_g(near, Y_UP), move_g(near, Y_DOWN)
        state = attend(pieces, masks, other, [(0, near[0], near[1])], [])
        onward = call(choose_kernel, sds(below.shape, BF16), [VM] * 2, VM, limit=4)(below, above)
        far = lax.ppermute(after(onward, *state), ("group", "tensor"), ONWARD)
        blocks = [(3, below[0], below[1]), (1, above[0], above[1])]
        state = attend(pieces, masks, other, blocks, state)
        blocks = [(2, far[0], far[1])]
        theirs = attend(pieces, masks, other, blocks, state, 1)[0]
        mine = attend(pieces, masks, other, blocks, state, 0)[0]
        attended = call(merge_kernel, [sds((HALF, HD), BF16)] * 4, [VM] * 2, [VM] * 4)(
            mine, swap(theirs)
        )
        if step == 0:
            out_weights = [output_weights, swap(after(output_weights, attended[0]))]
        attended = [attended[0]] + [move_g(attended[4 - j], Z_MOVES[4 - j]) for j in (1, 2, 3)]
        result = output(
            stack(attended, 0),
            out_weights,
            step,
            levels,
            group_order,
            step_sizes,
            dens,
            scales,
            tables,
        )
        if step < STEPS - 1:
            dens, shard = result[:2], result[2]
    return tuple(
        call(
            join_kernel,
            [sds((2 * HALF, FEAT), F32), sds((2 * HALF, FEAT), BF16)],
            [VM] * 2,
            [VM] * 2,
        )(result[1], swap(result[0]))
    )


def solution(mesh):
    placed = (
        P("group", "tensor"),
        P(None, None, "tensor"),
        P(None, "tensor"),
        P(None, "tensor"),
        P(None, "tensor"),
        P(),
        P("group", None),
        P("group"),
        P("group", None),
    )
    return jax.shard_map(
        body,
        mesh=mesh,
        in_specs=placed,
        out_specs=(P("group", "tensor"), P("group", "tensor")),
        check_vma=False,
    )
```
